256 devices in a mesh: slab: 16 (over z, core), clus: 16 (over y, x).
Axes of the slice: x: 4, y: 4, z: 8, core: 2. Of those that a mesh axis runs over, the one named last changes fastest.
Arguments:
- incident: float32 [8, 1024, 200], P(None, ('slab', 'clus')), may hold values from -6 to 6
- history: float32 [16, 1024, 200], P(None, ('slab', 'clus')), may hold values from -6 to 6
- near_blocks: bfloat16 [1024, 12, 200, 200], P(('slab', 'clus')), may hold values from -0.09375 to 0.09375
- near_idx: int32 [1024, 12], P(('slab', 'clus')), may hold values from 0 to 1023, as said below
- near_cnt: int32 [1024], P(('slab', 'clus')), may hold values from 3 to 12
- near_lag: int32 [1024, 12], P(('slab', 'clus')), may hold values from 1 to 15
- near_frac: float32 [1024, 12], P(('slab', 'clus')), may hold values from 0 to 1
- inverses: bfloat16 [1024, 200, 200], P(('slab', 'clus')), may hold values from -0.4375 to 0.4375
- rays: bfloat16 [1024, 512, 200], P(('slab', 'clus')), may hold values from -0.4375 to 0.4375
- shift: float32 [1024, 512], P(('slab', 'clus')), may hold values from -1 to 1
- far_idx: int32 [256, 8], replicated, may hold values from 0 to 255, as said below
- far_lag: int32 [256, 8], replicated, may hold values from 1 to 16
- trans: bfloat16 [256, 8, 512], replicated, may hold values from -0.5 to 0.5
Outputs:
- currents: float32 [8, 1024, 200], P(None, ('slab', 'clus'))
The draws below stay inside these ranges and needn't reach their ends.
Inputs may be any that keep to these rules, and one draw needn't show every extreme that they name: `near_idx`: every entry is a cluster whose slab (cluster number divided by 64) differs by at most one from the slab of the entry's row. `far_idx`: every entry is a group whose slab (group number divided by the number of devices along clus) differs by two or more from the slab of the entry's row.
All inputs are finite; a program needn't handle non-finite values.
Results may differ from the reference program's by a relative error of at most 0.0045.
Values sent between devices are 32-bit elements; how exact they have to be, the bound alone decides.
A program may use at most 128 MiB of HBM per device.

```python
import jax
import jax.numpy as jnp
from jax import lax

U = 200
DIR = 512
CL_DEV = 4
NB = 12
NF = 8
LAGS = 16
STEPS = 8
SLAB_CL = 64
GROUPS = 256
NC = 1024
N_SLAB = 16
N_CLUS = 16


def draw_near_idx(key, part):
    key = jax.random.fold_in(key, 7)
    first_key, second_key = jax.random.split(key)
    cluster = jnp.arange(NC, dtype=jnp.int32)[:, None]
    slab_of = cluster // SLAB_CL
    column = jnp.arange(NB, dtype=jnp.int32)[None, :]
    random_step = jax.random.randint(first_key, (NC, NB), -1, 2)
    offset = jnp.where(column == 0, 0, jnp.where(column == 1, -1, jnp.where(column == 2, 1, random_step)))
    target = jnp.clip(slab_of + offset, 0, N_SLAB - 1)
    member = jax.random.randint(second_key, (NC, NB), 0, SLAB_CL)
    return (target * SLAB_CL + member).astype(jnp.int32)


def draw_far_idx(key, part):
    key = jax.random.fold_in(key, 11)
    first_key, second_key = jax.random.split(key)
    own_slab = jnp.arange(GROUPS, dtype=jnp.int32)[:, None] // N_CLUS
    offset = jax.random.randint(first_key, (GROUPS, NF), 2, N_SLAB - 1)
    target = (own_slab + offset) % N_SLAB
    member = jax.random.randint(second_key, (GROUPS, NF), 0, N_CLUS)
    listed = (target * N_CLUS + member).astype(jnp.int32)
    return listed.at[0, 0].set(GROUPS - 1)


def place_ends(entries, rng, low, largest):
    spot = [jax.random.randint(jax.random.fold_in(rng, axis), (), 0, length) for axis, length in enumerate(entries.shape)]
    main_axis = entries.shape.index(max(entries.shape))
    beside = spot[:main_axis] + [(spot[main_axis] + 1) % entries.shape[main_axis]] + spot[main_axis + 1:]
    return entries.at[tuple(spot)].set(low).at[tuple(beside)].set(largest)


def shard_levels(own_key, shape, cuts, smallest, top_value):
    def one(position, shards_of):
        heights = jax.random.uniform(jax.random.fold_in(jax.random.fold_in(own_key, 6), position), (shards_of,), jnp.float32, smallest / len(cuts), top_value / len(cuts))
        return jnp.repeat(jnp.exp(heights), shape[position] // shards_of).reshape((-1,) + (1,) * (len(shape) - position - 1))

    loudness = one(*cuts[0])
    for cut in cuts[1:]:
        loudness = loudness * one(*cut)
    return loudness


def centred(key, dims, deviation, bound, cuts=(), kind=jnp.bfloat16):
    factor_of = shard_levels(key, dims, cuts, -0.22, 0.18) if cuts else 1.0
    array = jax.random.normal(key, dims, jnp.float32) * deviation * factor_of
    return jnp.minimum(jnp.maximum(array, -bound), bound).astype(kind)


def setup_inputs(seed: int = 0) -> dict:
    streams_of = jax.random.split(jax.random.key(seed), 14)
    incident = centred(streams_of[0], (STEPS, NC, U), 1.0, 6.0, ((1, 256),), jnp.float32)
    history = centred(streams_of[1], (LAGS, NC, U), 1.0, 6.0, ((1, 256),), jnp.float32)
    near_blocks = centred(streams_of[2], (NC, NB, U, U), (2 * U * NB) ** -0.5, 0.09375, ((0, 256),))
    near_idx = draw_near_idx(jax.random.fold_in(streams_of[13], 71), 0)
    near_cnt = place_ends(jax.random.randint(streams_of[4], (NC,), 3, NB + 1), jax.random.fold_in(streams_of[4], 1), 3, NB).astype(jnp.int32)
    near_lag = place_ends(jax.random.randint(streams_of[5], (NC, NB), 1, LAGS), jax.random.fold_in(streams_of[5], 1), 1, LAGS - 1).astype(jnp.int32)
    near_frac = jnp.clip(1.0 * jax.random.uniform(streams_of[6], (NC, NB), jnp.float32) ** shard_levels(streams_of[6], (NC, NB), ((0, 256),), -0.2, 0.2), 0.0, 1.0)
    inverses = centred(streams_of[7], (NC, U, U), U ** -0.5, 0.4375, ((0, 256),))
    rays = centred(streams_of[8], (NC, DIR, U), U ** -0.5, 0.4375, ((0, 256),))
    shift = jnp.clip(jax.random.uniform(streams_of[9], (NC, DIR), jnp.float32, -1.0, 1.0) * shard_levels(streams_of[9], (NC, DIR), ((0, 256),), -0.4, 0.0), -1.0, 1.0)
    far_idx = draw_far_idx(jax.random.fold_in(streams_of[13], 71), 0)
    far_lag = place_ends(jax.random.randint(streams_of[11], (GROUPS, NF), 1, LAGS + 1), jax.random.fold_in(streams_of[11], 1), 1, LAGS).astype(jnp.int32)
    trans = centred(streams_of[12], (GROUPS, NF, DIR), (4 * NF * CL_DEV) ** -0.5, 0.5)
    return {"incident": incident, "history": history, "near_blocks": near_blocks, "near_idx": near_idx, "near_cnt": near_cnt, "near_lag": near_lag, "near_frac": near_frac, "inverses": inverses, "rays": rays, "shift": shift, "far_idx": far_idx, "far_lag": far_lag, "trans": trans}


def rounded(value):
    return lax.optimization_barrier(value.astype(jnp.bfloat16)).astype(jnp.float32)


def group_spectra(rays, shift, current):
    def one_group(pieces):
        ray_block, shift_block, cur_block = pieces
        ray_vals = jnp.einsum("cdu,cu->cd", ray_block.astype(jnp.float32), rounded(cur_block))
        return jnp.sum(ray_vals * shift_block, axis=0)
    return lax.map(one_group, (rays.reshape(GROUPS, CL_DEV, DIR, U), shift.reshape(GROUPS, CL_DEV, DIR), current.reshape(GROUPS, CL_DEV, U)))


def reference(incident, history, near_blocks, near_idx, near_cnt, near_lag, near_frac, inverses, rays, shift, far_idx, far_lag, trans):
    timeline = jnp.concatenate([history, jnp.zeros((STEPS, NC, U), jnp.float32)], axis=0)
    spec_hist = jnp.stack([group_spectra(rays, shift, history[k]) for k in range(LAGS)], axis=0)
    spec_time = jnp.concatenate([spec_hist, jnp.zeros((STEPS, GROUPS, DIR), jnp.float32)], axis=0)
    live_slot = jnp.arange(NB)[None, :] < near_cnt[:, None]
    near_weight = near_frac[..., None]
    trans_wide = trans.astype(jnp.float32)
    blocks_shaped = near_blocks.reshape(GROUPS, CL_DEV, NB, U, U)
    rays_shaped = rays.reshape(GROUPS, CL_DEV, DIR, U)
    inverse_shaped = inverses.reshape(GROUPS, CL_DEV, U, U)
    outputs = []
    for step_index in range(STEPS):
        lag_slot = step_index - near_lag + LAGS
        first_lag = timeline[lag_slot, near_idx]
        second = timeline[lag_slot - 1, near_idx]
        blended = jnp.where(live_slot[..., None], (1.0 - near_weight) * first_lag + near_weight * second, 0.0)

        def near_group(pieces):
            block, vector = pieces
            return jnp.einsum("cjuv,cjv->cu", block.astype(jnp.float32), rounded(vector))
        near_field = lax.map(near_group, (blocks_shaped, blended.reshape(GROUPS, CL_DEV, NB, U))).reshape(NC, U)
        far_slot = step_index - far_lag + LAGS
        picked = spec_time[far_slot, far_idx]
        incoming = jnp.sum(trans_wide * picked, axis=1)
        inbound = jnp.repeat(incoming, CL_DEV, axis=0) * shift

        def far_group(pieces):
            ray_block, vector = pieces
            return jnp.einsum("cdu,cd->cu", ray_block.astype(jnp.float32), rounded(vector))
        far_field = lax.map(far_group, (rays_shaped, inbound.reshape(GROUPS, CL_DEV, DIR))).reshape(NC, U)
        right_side = incident[step_index] - near_field - far_field

        def solve_group(pieces):
            block, vector = pieces
            return jnp.einsum("cuv,cv->cu", block.astype(jnp.float32), rounded(vector))
        current = lax.map(solve_group, (inverse_shaped, right_side.reshape(GROUPS, CL_DEV, U))).reshape(NC, U)
        outputs.append(current)
        timeline = timeline.at[LAGS + step_index].set(current)
        spec_time = spec_time.at[LAGS + step_index].set(group_spectra(rays, shift, current))
    return jnp.stack(outputs, axis=0)
```

```python
import functools

import jax
import jax.numpy as jnp
from jax import lax
from jax.experimental import pallas as pl
from jax.experimental.pallas import tpu as pltpu
from jax.sharding import PartitionSpec as P

MESH = pl.DeviceIdType.MESH
LANES = 128
CHUNK = 32
NT = (((1,), (1,)), ((), ()))
NN = (((1,), (0,)), ((), ()))


def dot(left, right, dims):
    return lax.dot_general(left, right, dims, preferred_element_type=jnp.float32)


def remote(src, dst, send, recv, device):
    return pltpu.make_async_remote_copy(
        src_ref=src, dst_ref=dst, send_sem=send, recv_sem=recv,
        device_id=device, device_id_type=MESH,
    )


def march(
    sizes,
    near_row, near_sub, near_now, near_old, far_row,
    incident, message0, rays, shift, inverses, far_weight, fresh_weight, near_hbm,
    out,
    near, line, land, spectra, part_out, part_in, early, blend, partial, incoming,
    near_sem, hist_send, hist_recv, wide_send, wide_recv,
    one_send, one_recv, fwd_send, fwd_recv, two_send, two_recv,
):
    steps, lags, n_slab, n_clus, per, slots, unknowns, far_slots = sizes
    span = lags + steps
    slab = lax.axis_index("slab")
    clus = lax.axis_index("clus")
    after = lax.rem(slab + 1, n_slab)
    before = lax.rem(slab + n_slab - 1, n_slab)
    tail = unknowns - LANES
    quarters = shift.shape[1] // LANES
    home = n_clus + clus

    fetch = pltpu.make_async_copy(near_hbm, near, near_sem)
    fetch.start()

    barrier = pltpu.get_barrier_semaphore()

    def greet_plane(k, carry):
        pl.semaphore_signal(barrier, inc=1, device_id=(slab, lax.rem(clus + k, n_clus)), device_id_type=MESH)
        return carry

    def greet_column(k, carry):
        pl.semaphore_signal(barrier, inc=1, device_id=(lax.rem(slab + k, n_slab), clus), device_id_type=MESH)
        return carry

    lax.fori_loop(1, n_clus, greet_plane, 0)
    lax.fori_loop(1, n_slab, greet_column, 0)
    line[home, pl.ds(0, lags)] = message0[...]
    pl.semaphore_wait(barrier, n_clus + n_slab - 2)

    def hist_start(k, carry):
        piece = line.at[home, pl.ds(0, lags)]
        remote(piece, piece, hist_send, hist_recv.at[clus], (slab, lax.rem(clus + k, n_clus))).start()
        return carry

    lax.fori_loop(1, n_clus, hist_start, 0)

    def wide_start(k):
        source = n_clus + k
        piece = line.at[source, pl.ds(0, lags), pl.ds(0, 2)]
        remote(piece, line.at[k + 2 * n_clus, pl.ds(0, lags), pl.ds(0, 2)],
               wide_send.at[0], wide_recv.at[0], (before, clus)).start()
        remote(piece, line.at[k, pl.ds(0, lags), pl.ds(0, 2)],
               wide_send.at[1], wide_recv.at[1], (after, clus)).start()

    wide_start(clus)

    def hist_next(k, carry):
        source = lax.rem(clus + k, n_clus)
        piece = line.at[n_clus + source, pl.ds(0, lags)]
        remote(piece, piece, hist_send, hist_recv.at[source], (slab, clus)).wait_recv()
        wide_start(source)
        return carry

    lax.fori_loop(1, n_clus, hist_next, 0)

    def whole_wide(which):
        piece = line.at[pl.ds(0, n_clus), pl.ds(0, lags), pl.ds(0, 2)]
        return remote(piece, piece, wide_send.at[which], wide_recv.at[which], (slab, clus))

    def far_early(step):
        def one(target, carry):
            total = jnp.zeros((quarters, LANES), jnp.float32)
            for slot in range(far_slots):
                entry = target * far_slots + slot
                row = far_row[step * (n_slab * far_slots) + entry]
                total += far_weight[entry] * line[lax.div(row, span), lax.rem(row, span), 2]
            early[target] = total
            return carry

        lax.fori_loop(0, n_slab, one, 0)

    whole_wide(0).wait_recv()
    whole_wide(1).wait_recv()
    far_early(0)
    fetch.wait()

    row_id = lax.broadcasted_iota(jnp.int32, (per, 1), 0)

    def whole_one(step):
        piece = land.at[step, pl.ds(0, n_clus - 1)]
        return remote(piece, piece, one_send.at[step], one_recv.at[step], (slab, clus))

    def whole_fwd(step, which):
        piece = land.at[step, pl.ds(0, n_clus), pl.ds(0, 2)]
        return remote(piece, piece, fwd_send.at[step, which], fwd_recv.at[step, which], (slab, clus))

    def whole_two(step):
        piece = part_in.at[step, pl.ds(0, n_slab - 1)]
        return remote(piece, piece, two_send.at[step], two_recv.at[step], (slab, clus))

    def body(step, carry):
        totals = [
            jnp.concatenate([early[2 * p], early[2 * p + 1]], axis=0) for p in range(n_slab // 2)
        ]
        for member in range(n_clus):
            one = line[n_clus + member, lags - 1 + step, 2]
            both = jnp.concatenate([one, one], axis=0)
            for p in range(n_slab // 2):
                totals[p] += fresh_weight[member, p] * both
        for p in range(n_slab // 2):
            part_out[step, 2 * p] = totals[p][:quarters]
            part_out[step, 2 * p + 1] = totals[p][quarters:]

        def two_start(k, inner):
            target = lax.rem(slab + k, n_slab)
            remote(part_out.at[step, target], part_in.at[step, slab],
                   two_send.at[step], two_recv.at[step], (target, clus)).start()
            return inner

        lax.fori_loop(1, n_slab, two_start, 0)
        part_in[step, slab] = part_out[step, slab]

        @pl.when(step > 0)
        def _():
            past = step - 1
            for which, first in ((0, 2 * n_clus), (1, 0)):
                whole_fwd(past, which).wait_recv()
                for k in range(n_clus):
                    line[first + k, lags + past, pl.ds(0, 2)] = land[past, first + k, pl.ds(0, 2)]

        def blend_one(entry, inner):
            row = near_row[step * (per * slots) + entry]
            sub = near_sub[entry]
            device, time = lax.div(row, span), lax.rem(row, span)
            now, old = near_now[entry], near_old[entry]
            for half in range(2):
                mixed = (
                    now * line[device, time + 1, half, pl.ds(sub, 1), :]
                    + old * line[device, time, half, pl.ds(sub, 1), :]
                )
                blend[half, pl.ds(entry, 1), :] = mixed.astype(jnp.bfloat16).astype(jnp.float32)
            return inner

        lax.fori_loop(0, per * slots, blend_one, 0, unroll=4)

        def near_one(c, inner):
            for first in range(0, unknowns, CHUNK):
                rows = min(CHUNK, unknowns - first)
                left = jnp.zeros((rows, LANES), jnp.float32)
                right = jnp.zeros((rows, tail), jnp.float32)
                for j in range(slots):
                    entry = c * slots + j
                    left += (near[c, j, pl.ds(first, rows), pl.ds(0, LANES)].astype(jnp.float32)
                             * blend[0, pl.ds(entry, 1), :])
                    right += (near[c, j, pl.ds(first, rows), pl.ds(LANES, tail)].astype(jnp.float32)
                              * blend[1, pl.ds(entry, 1), pl.ds(0, tail)])
                partial[c, pl.ds(first, rows), :] = left + jnp.concatenate(
                    [right, jnp.zeros((rows, LANES - tail), jnp.float32)], axis=1)
            return inner

        lax.fori_loop(0, per, near_one, 0)

        field = jnp.zeros((per, unknowns), jnp.float32)
        for c in range(per):
            pick = jnp.where(row_id == c, 1.0, 0.0) * jnp.ones((per, LANES), jnp.float32)
            pick = pick.astype(jnp.bfloat16)
            value = partial[c]
            high = value.astype(jnp.bfloat16)
            low = (value - high.astype(jnp.float32)).astype(jnp.bfloat16)
            field += dot(pick, high, NT) + dot(pick, low, NT)

        whole_two(step).wait_recv()
        incoming[...] = jnp.sum(part_in[step], axis=0)
        spread = jnp.concatenate(
            [shift[:, q * LANES:(q + 1) * LANES] * incoming[pl.ds(q, 1), :] for q in range(quarters)], axis=1)
        for c in range(per):
            field += dot(jnp.where(row_id == c, spread, 0.0).astype(jnp.bfloat16), rays[c], NN)
        right_side = (incident[step] - field).astype(jnp.bfloat16).astype(jnp.float32)
        current = jnp.zeros((per, unknowns), jnp.float32)
        for c in range(per):
            current += dot(jnp.where(row_id == c, right_side, 0.0).astype(jnp.bfloat16), inverses[c], NT)
        out[step] = current

        @pl.when(step < steps - 1)
        def _():
            rounded = current.astype(jnp.bfloat16).astype(jnp.float32)
            values = jnp.zeros((per, quarters * LANES), jnp.float32)
            for c in range(per):
                values += dot(jnp.where(row_id == c, rounded, 0.0).astype(jnp.bfloat16), rays[c], NT)
            spectrum = jnp.sum(values * shift[...], axis=0, keepdims=True)
            land[step, home, 0] = current[:, :LANES]
            land[step, home, 1] = jnp.concatenate(
                [current[:, LANES:], jnp.zeros((per, LANES - tail), jnp.float32)], axis=1)
            for q in range(quarters):
                land[step, home, 2, pl.ds(q, 1), :] = spectrum[:, q * LANES:(q + 1) * LANES]

            def one_start(k, inner):
                piece = land.at[step, home]
                remote(piece, piece, one_send.at[step], one_recv.at[step],
                       (slab, lax.rem(clus + k, n_clus))).start()
                return inner

            lax.fori_loop(1, n_clus, one_start, 0)
            far_early(step + 1)
            whole_one(step).wait_recv()
            piece = land.at[step, pl.ds(n_clus, n_clus), pl.ds(0, 2)]
            remote(piece, land.at[step, pl.ds(2 * n_clus, n_clus), pl.ds(0, 2)],
                   fwd_send.at[step, 0], fwd_recv.at[step, 0], (before, clus)).start()
            remote(piece, land.at[step, pl.ds(0, n_clus), pl.ds(0, 2)],
                   fwd_send.at[step, 1], fwd_recv.at[step, 1], (after, clus)).start()
            for k in range(n_clus):
                line[n_clus + k, lags + step] = land[step, n_clus + k]

        return carry

    lax.fori_loop(0, steps, body, 0)

    piece = line.at[pl.ds(0, n_clus - 1), pl.ds(0, lags)]
    remote(piece, piece, hist_send, hist_send, (slab, clus)).wait_send()
    whole_wide(0).wait_send()
    whole_wide(1).wait_send()

    def finish(step, carry):
        whole_two(step).wait_send()

        @pl.when(step < steps - 1)
        def _():
            whole_one(step).wait_send()
            whole_fwd(step, 0).wait_send()
            whole_fwd(step, 1).wait_send()

        return carry

    lax.fori_loop(0, steps, finish, 0)


def local(
    incident, history, near_blocks, near_idx, near_cnt, near_lag, near_frac,
    inverses, rays, shift, far_idx, far_lag, trans,
):
    lags, per, unknowns = history.shape
    steps = incident.shape[0]
    dirs = rays.shape[1]
    slots = near_idx.shape[1]
    far_slots = far_idx.shape[1]
    n_slab = lax.axis_size("slab")
    n_clus = lax.axis_size("clus")
    span = lags + steps
    quarters = dirs // LANES
    slab = lax.axis_index("slab")
    clus = lax.axis_index("clus")
    times = jnp.arange(steps, dtype=jnp.int32)

    past_rays = jnp.einsum("cdu,tcu->tcd", rays, history.astype(jnp.bfloat16), preferred_element_type=jnp.float32)
    past = jnp.sum(past_rays * shift[None], axis=1).reshape(lags, 1, quarters, LANES)
    padded = jnp.pad(history, ((0, 0), (0, 0), (0, 2 * LANES - unknowns)))
    halves = padded.reshape(lags, per, 2, LANES).transpose(0, 2, 1, 3)
    message0 = jnp.concatenate([halves, past], axis=1)

    near_local = near_idx - (slab - 1) * (n_clus * per)
    live = jnp.arange(slots)[None, :] < near_cnt[:, None]
    near_base = (near_local // per) * span + lags - 1 - near_lag
    near_row = (times[:, None] + near_base.reshape(1, -1)).reshape(-1)
    near_sub = (near_local % per).reshape(-1)
    near_now = jnp.where(live, 1.0 - near_frac, 0.0).reshape(-1)
    near_old = jnp.where(live, near_frac, 0.0).reshape(-1)

    def column(table):
        shaped = table.reshape((n_slab, n_clus) + table.shape[1:])
        return lax.dynamic_index_in_dim(shaped, clus, 1, keepdims=False)

    idx, lag, weight = column(far_idx), column(far_lag), column(trans)
    mine = idx // n_clus == slab
    member = idx % n_clus
    old = mine & (lag >= 2)
    base = jnp.where(old, (n_clus + member) * span + lags - lag, n_clus * span)
    far_row = (base.reshape(1, -1) + jnp.where(old.reshape(1, -1), times[:, None], 0)).reshape(-1)
    far_weight = jnp.where(old[..., None], weight.astype(jnp.float32), 0.0).reshape(-1, quarters, LANES)
    newest = mine & (lag == 1)
    onehot = (newest[..., None] & (member[..., None] == jnp.arange(n_clus))).astype(jnp.bfloat16)
    fresh = jnp.einsum("tjm,tjd->mtd", onehot, weight, preferred_element_type=jnp.float32)
    fresh_weight = fresh.reshape(n_clus, n_slab // 2, 2 * quarters, LANES)

    sizes = (steps, lags, n_slab, n_clus, per, slots, unknowns, far_slots)
    smem = pl.BlockSpec(memory_space=pltpu.SMEM)
    vmem = pl.BlockSpec(memory_space=pltpu.VMEM)
    dma = pltpu.SemaphoreType.DMA
    devices = 3 * n_clus
    return pl.pallas_call(
        functools.partial(march, sizes),
        out_shape=jax.ShapeDtypeStruct((steps, per, unknowns), jnp.float32),
        in_specs=[smem] * 5 + [vmem] * 7 + [pl.BlockSpec(memory_space=pl.ANY)],
        out_specs=vmem,
        scratch_shapes=[
            pltpu.VMEM(near_blocks.shape, near_blocks.dtype),
            pltpu.VMEM((devices, span, 3, per, LANES), jnp.float32),
            pltpu.VMEM((steps - 1, devices, 3, per, LANES), jnp.float32),
            pltpu.VMEM((8, LANES), jnp.float32),
            pltpu.VMEM((steps, n_slab, quarters, LANES), jnp.float32),
            pltpu.VMEM((steps, n_slab, quarters, LANES), jnp.float32),
            pltpu.VMEM((n_slab, quarters, LANES), jnp.float32),
            pltpu.VMEM((2, per * slots, LANES), jnp.float32),
            pltpu.VMEM((per, unknowns, LANES), jnp.float32),
            pltpu.VMEM((quarters, LANES), jnp.float32),
            dma(()), dma(()), dma((n_clus,)), dma((2,)), dma((2,)),
            dma((steps - 1,)), dma((steps - 1,)), dma((steps - 1, 2)), dma((steps - 1, 2)),
            dma((steps,)), dma((steps,)),
        ],
        compiler_params=pltpu.CompilerParams(
            collective_id=0, has_side_effects=True, vmem_limit_bytes=48 * 1024 * 1024
        ),
    )(
        near_row, near_sub, near_now, near_old, far_row,
        incident, message0, rays, shift, inverses, far_weight, fresh_weight, near_blocks,
    )


def solution(mesh):
    split = ("slab", "clus")
    in_specs = (
        P(None, split, None),
        P(None, split, None),
        P(split, None, None, None),
        P(split, None),
        P(split),
        P(split, None),
        P(split, None),
        P(split, None, None),
        P(split, None, None),
        P(split, None),
        P(),
        P(),
        P(),
    )
    return jax.shard_map(local, mesh=mesh, in_specs=in_specs, out_specs=P(None, split, None), check_vma=False)
```

```python
import functools

import jax
import jax.numpy as jnp
from jax import lax
from jax.experimental import pallas as pl
from jax.experimental.pallas import tpu as pltpu
from jax.sharding import PartitionSpec as P

MESH = pl.DeviceIdType.MESH
LANES = 128
CHUNK = 32
SIDE = 4
FAR_FIRST = (
    (2, 2), (2, 1), (2, 3), (1, 2), (3, 2), (2, 0), (0, 2), (1, 1),
    (1, 3), (3, 1), (3, 3), (1, 0), (3, 0), (0, 1), (0, 3),
)
NT = (((1,), (1,)), ((), ()))
NN = (((1,), (0,)), ((), ()))


def dot(left, right, dims):
    return lax.dot_general(left, right, dims, preferred_element_type=jnp.float32)


def remote(src, dst, send, recv, device):
    return pltpu.make_async_remote_copy(
        src_ref=src, dst_ref=dst, send_sem=send, recv_sem=recv,
        device_id=device, device_id_type=MESH,
    )


def march(
    sizes,
    near_idx, near_cnt, near_lag, near_frac, far_code,
    incident, history, rays, shift, inverses, far_weight, fresh_weight, near_hbm,
    out,
    near, line, past, land, part_out, part_in, early, blend, partial, incoming,
    near_sem, ray_send, ray_recv, ray_far_recv, cur_send, cur_recv, cur_far_recv, wide_send, wide_recv,
    one_send, one_recv, fwd_send, fwd_recv, two_send, two_recv,
):
    steps, lags, n_slab, side, per, slots, unknowns, far_slots = sizes
    n_clus = side * side
    middle = lags // 2
    slab = lax.axis_index("slab")
    clus = lax.axis_index("clus")
    row, col = clus // side, lax.rem(clus, side)
    after = lax.rem(slab + 1, n_slab)
    before = lax.rem(slab + n_slab - 1, n_slab)
    tail = unknowns - LANES
    quarters = shift.shape[1] // LANES
    home = n_clus + clus
    early_half, late_half = pl.ds(0, middle), pl.ds(middle, lags - middle)

    barrier = pltpu.get_barrier_semaphore()

    def greet_plane(k, carry):
        pl.semaphore_signal(barrier, inc=1, device_id=(slab, lax.rem(clus + k, n_clus)), device_id_type=MESH)
        return carry

    def greet_column(k, carry):
        pl.semaphore_signal(barrier, inc=1, device_id=(lax.rem(slab + k, n_slab), clus), device_id_type=MESH)
        return carry

    lax.fori_loop(1, n_clus, greet_plane, 0)
    lax.fori_loop(1, n_slab, greet_column, 0)
    fetch = pltpu.make_async_copy(near_hbm, near, near_sem)
    fetch.start()

    line[1, row, col, pl.ds(0, lags), 0] = history[:, :, :LANES]
    line[1, row, col, pl.ds(0, lags), 1] = jnp.concatenate(
        [history[:, :, LANES:], jnp.zeros((lags, per, LANES - tail), jnp.float32)], axis=2)
    spectra = jnp.zeros((lags, quarters * LANES), jnp.float32)
    for c in range(per):
        spectra += dot(history[:, c, :].astype(jnp.bfloat16), rays[c], NT) * shift[c:c + 1, :]
    for q in range(quarters):
        past[row, col, pl.ds(0, lags), q, :] = spectra[:, q * LANES:(q + 1) * LANES]
    pl.semaphore_wait(barrier, n_clus + n_slab - 2)

    def along_x(k):
        return (slab, row * side + lax.rem(col + k, side))

    def along_y(k):
        return (slab, lax.rem(row + k, side) * side + col)

    own_ray = [past.at[row, col, early_half], past.at[row, col, late_half]]
    own_cur = [line.at[1, row, col, early_half], line.at[1, row, col, late_half]]
    row_ray = [past.at[row, :, early_half], past.at[:, col, late_half]]

    def cur_strip(which, place):
        return line.at[1, place, :, early_half] if which == 0 else line.at[1, :, place, late_half]

    toward = [along_x, along_y]
    place = [row, col]
    for own, send, recv in ((own_ray, ray_send, ray_recv), (own_cur, cur_send, cur_recv)):
        for which in range(2):
            for k in (2, 1, 3):
                remote(own[which], own[which], send.at[0, which], recv.at[which], toward[which](k)).start()

    three_ray = [past.at[0, pl.ds(0, side - 1), early_half], past.at[0, pl.ds(0, side - 1), late_half]]
    three_cur = [line.at[1, 0, pl.ds(0, side - 1), early_half], line.at[1, 0, pl.ds(0, side - 1), late_half]]
    strips_ray = [past.at[pl.ds(0, side - 1), :, early_half], past.at[pl.ds(0, side - 1), :, late_half]]
    strips_cur = [line.at[1, pl.ds(0, side - 1), :, early_half], line.at[1, pl.ds(0, side - 1), :, late_half]]

    def waiter(piece, send, recv):
        return remote(piece, piece, send, recv, (slab, clus))

    for which in range(2):
        waiter(three_ray[which], ray_send.at[0, which], ray_recv.at[which]).wait_recv()
        for k in (2, 1, 3):
            remote(row_ray[which], row_ray[which], ray_send.at[1, which], ray_far_recv.at[which],
                   toward[1 - which](k)).start()

    def wide_start(which, spot):
        piece = cur_strip(which, spot)
        for side_of, device, slot in ((0, before, 2), (1, after, 0)):
            target = line.at[slot, spot, :, early_half] if which == 0 else line.at[slot, :, spot, late_half]
            remote(piece, target, wide_send.at[side_of], wide_recv.at[side_of], (device, clus)).start()

    for which in range(2):
        waiter(three_cur[which], cur_send.at[0, which], cur_recv.at[which]).wait_recv()
        strip = cur_strip(which, place[which])
        for k in (2, 1, 3):
            remote(strip, strip, cur_send.at[1, which], cur_far_recv.at[which, place[which]],
                   toward[1 - which](k)).start()
        wide_start(which, place[which])

    def whole_wide(which):
        piece = line.at[0, :, :, pl.ds(0, lags)]
        return waiter(piece, wide_send.at[which], wide_recv.at[which])

    def far_early(step):
        def one(target, carry):
            total = jnp.zeros((quarters, LANES), jnp.float32)
            for slot in range(far_slots):
                entry = target * far_slots + slot
                code = far_code[entry]
                group, lag = lax.div(code, 32), lax.rem(code, 32)
                member = lax.rem(group, n_clus)
                old = lag >= 2
                time = jnp.where(old, step + lags - lag, 0)
                mine = jnp.where(old & (lax.div(group, n_clus) == slab), 1.0, 0.0)
                total += (far_weight[entry] * mine) * past[lax.div(member, side), lax.rem(member, side), time]
            early[target] = total
            return carry

        lax.fori_loop(0, n_slab, one, 0)

    def far_send(step):
        totals = [
            jnp.concatenate([early[2 * p], early[2 * p + 1]], axis=0) for p in range(n_slab // 2)
        ]
        for member in range(n_clus):
            one = past[member // side, member % side, lags - 1 + step]
            both = jnp.concatenate([one, one], axis=0)
            for p in range(n_slab // 2):
                totals[p] += fresh_weight[member, p] * both
        for p in range(n_slab // 2):
            part_out[step, 2 * p] = totals[p][:quarters]
            part_out[step, 2 * p + 1] = totals[p][quarters:]

        def two_start(k, inner):
            target = lax.rem(slab + k, n_slab)
            remote(part_out.at[step, target], part_in.at[step, slab],
                   two_send.at[step], two_recv.at[step], (target, clus)).start()
            return inner

        lax.fori_loop(1, n_slab, two_start, 0)
        part_in[step, slab] = part_out[step, slab]

    for which in range(2):
        waiter(strips_ray[which], ray_send.at[1, which], ray_far_recv.at[which]).wait_recv()
    far_early(0)
    far_send(0)

    for k in (1, 3, 2):
        for which in range(2):
            spot = lax.rem(place[which] + k, side)
            waiter(cur_strip(which, spot), cur_send.at[1, which], cur_far_recv.at[which, spot]).wait_recv()
            wide_start(which, spot)

    whole_wide(0).wait_recv()
    whole_wide(1).wait_recv()
    fetch.wait()

    row_id = lax.broadcasted_iota(jnp.int32, (per, 1), 0)

    def whole_one(step):
        return waiter(land.at[step, pl.ds(0, n_clus - 1)], one_send.at[step], one_recv.at[step])

    def whole_fwd(step, which):
        return waiter(land.at[step, pl.ds(0, n_clus), pl.ds(0, 2)], fwd_send.at[step, which], fwd_recv.at[step, which])

    def whole_two(step):
        return waiter(part_in.at[step, pl.ds(0, n_slab - 1)], two_send.at[step], two_recv.at[step])

    def body(step, carry):
        @pl.when(step > 0)
        def _():
            last = step - 1
            for which, slot in ((0, 2), (1, 0)):
                whole_fwd(last, which).wait_recv()
                for k in range(n_clus):
                    line[slot, k // side, k % side, lags + last] = land[last, slot * n_clus + k, pl.ds(0, 2)]

        def blend_one(c, inner):
            for j in range(slots):
                entry = c * slots + j
                local_idx = jnp.clip(near_idx[c, j] - (slab - 1) * (n_clus * per), 0, 3 * n_clus * per - 1)
                device, sub = lax.div(local_idx, per), lax.rem(local_idx, per)
                spot = lax.rem(device, n_clus)
                index = (lax.div(device, n_clus), lax.div(spot, side), lax.rem(spot, side))
                time = step + lags - 1 - near_lag[c, j]
                live = j < near_cnt[c]
                now = jnp.where(live, 1.0 - near_frac[c, j], 0.0)
                old = jnp.where(live, near_frac[c, j], 0.0)
                for half in range(2):
                    mixed = (
                        now * line[index + (time + 1, half, pl.ds(sub, 1), slice(None))]
                        + old * line[index + (time, half, pl.ds(sub, 1), slice(None))]
                    )
                    blend[half, pl.ds(entry, 1), :] = mixed.astype(jnp.bfloat16).astype(jnp.float32)
            return inner

        lax.fori_loop(0, per, blend_one, 0)

        def near_one(c, inner):
            for first in range(0, unknowns, CHUNK):
                rows = min(CHUNK, unknowns - first)
                left = jnp.zeros((rows, LANES), jnp.float32)
                right = jnp.zeros((rows, tail), jnp.float32)
                for j in range(slots):
                    entry = c * slots + j
                    left += (near[c, j, pl.ds(first, rows), pl.ds(0, LANES)].astype(jnp.float32)
                             * blend[0, pl.ds(entry, 1), :])
                    right += (near[c, j, pl.ds(first, rows), pl.ds(LANES, tail)].astype(jnp.float32)
                              * blend[1, pl.ds(entry, 1), pl.ds(0, tail)])
                partial[c, pl.ds(first, rows), :] = left + jnp.concatenate(
                    [right, jnp.zeros((rows, LANES - tail), jnp.float32)], axis=1)
            return inner

        lax.fori_loop(0, per, near_one, 0)

        field = jnp.zeros((per, unknowns), jnp.float32)
        for c in range(per):
            pick = jnp.where(row_id == c, 1.0, 0.0) * jnp.ones((per, LANES), jnp.float32)
            pick = pick.astype(jnp.bfloat16)
            value = partial[c]
            high = value.astype(jnp.bfloat16)
            low = (value - high.astype(jnp.float32)).astype(jnp.bfloat16)
            field += dot(pick, high, NT) + dot(pick, low, NT)

        whole_two(step).wait_recv()
        incoming[...] = jnp.sum(part_in[step], axis=0)
        spread = jnp.concatenate(
            [shift[:, q * LANES:(q + 1) * LANES] * incoming[pl.ds(q, 1), :] for q in range(quarters)], axis=1)
        for c in range(per):
            field += dot(jnp.where(row_id == c, spread, 0.0).astype(jnp.bfloat16), rays[c], NN)
        right_side = (incident[step] - field).astype(jnp.bfloat16).astype(jnp.float32)
        current = jnp.zeros((per, unknowns), jnp.float32)
        for c in range(per):
            current += dot(jnp.where(row_id == c, right_side, 0.0).astype(jnp.bfloat16), inverses[c], NT)
        out[step] = current

        @pl.when(step < steps - 1)
        def _():
            rounded = current.astype(jnp.bfloat16).astype(jnp.float32)
            values = jnp.zeros((per, quarters * LANES), jnp.float32)
            for c in range(per):
                values += dot(jnp.where(row_id == c, rounded, 0.0).astype(jnp.bfloat16), rays[c], NT)
            spectrum = jnp.sum(values * shift[...], axis=0, keepdims=True)
            land[step, home, 0] = current[:, :LANES]
            land[step, home, 1] = jnp.concatenate(
                [current[:, LANES:], jnp.zeros((per, LANES - tail), jnp.float32)], axis=1)
            for q in range(quarters):
                land[step, home, 2, pl.ds(q, 1), :] = spectrum[:, q * LANES:(q + 1) * LANES]

            for dy, dx in FAR_FIRST:
                piece = land.at[step, home]
                target = lax.rem(row + dy, side) * side + lax.rem(col + dx, side)
                remote(piece, piece, one_send.at[step], one_recv.at[step], (slab, target)).start()

            far_early(step + 1)
            whole_one(step).wait_recv()
            piece = land.at[step, pl.ds(n_clus, n_clus), pl.ds(0, 2)]
            remote(piece, land.at[step, pl.ds(2 * n_clus, n_clus), pl.ds(0, 2)],
                   fwd_send.at[step, 0], fwd_recv.at[step, 0], (before, clus)).start()
            remote(piece, land.at[step, pl.ds(0, n_clus), pl.ds(0, 2)],
                   fwd_send.at[step, 1], fwd_recv.at[step, 1], (after, clus)).start()
            for k in range(n_clus):
                past[k // side, k % side, lags + step] = land[step, n_clus + k, 2]
            far_send(step + 1)
            for k in range(n_clus):
                line[1, k // side, k % side, lags + step] = land[step, n_clus + k, pl.ds(0, 2)]

        return carry

    lax.fori_loop(0, steps, body, 0)

    for which in range(2):
        waiter(three_ray[which], ray_send.at[0, which], ray_recv.at[which]).wait_send()
        waiter(three_cur[which], cur_send.at[0, which], cur_recv.at[which]).wait_send()
        waiter(strips_ray[which], ray_send.at[1, which], ray_recv.at[which]).wait_send()
        waiter(strips_cur[which], cur_send.at[1, which], cur_recv.at[which]).wait_send()
        whole_wide(which).wait_send()

    def finish(step, carry):
        whole_two(step).wait_send()

        @pl.when(step < steps - 1)
        def _():
            whole_one(step).wait_send()
            whole_fwd(step, 0).wait_send()
            whole_fwd(step, 1).wait_send()

        return carry

    lax.fori_loop(0, steps, finish, 0)


def local(
    incident, history, near_blocks, near_idx, near_cnt, near_lag, near_frac,
    inverses, rays, shift, far_idx, far_lag, trans,
):
    lags, per, unknowns = history.shape
    steps = incident.shape[0]
    slots = near_idx.shape[1]
    far_slots = far_idx.shape[1]
    n_slab = lax.axis_size("slab")
    n_clus = lax.axis_size("clus")
    side = SIDE
    span = lags + steps
    quarters = rays.shape[1] // LANES
    slab = lax.axis_index("slab")
    clus = lax.axis_index("clus")

    def column(table):
        shaped = table.reshape((n_slab, n_clus) + table.shape[1:])
        return lax.dynamic_index_in_dim(shaped, clus, 1, keepdims=False)

    code = column(far_idx * 32 + far_lag)
    idx, lag, weight = code // 32, code % 32, column(trans)
    far_weight = weight.astype(jnp.float32).reshape(-1, quarters, LANES)
    newest = (idx // n_clus == slab) & (lag == 1)
    onehot = (newest[..., None] & (idx[..., None] % n_clus == jnp.arange(n_clus))).astype(jnp.bfloat16)
    fresh = jnp.einsum("tjm,tjd->mtd", onehot, weight, preferred_element_type=jnp.float32)
    fresh_weight = fresh.reshape(n_clus, n_slab // 2, 2 * quarters, LANES)

    sizes = (steps, lags, n_slab, side, per, slots, unknowns, far_slots)
    smem = pl.BlockSpec(memory_space=pltpu.SMEM)
    vmem = pl.BlockSpec(memory_space=pltpu.VMEM)
    dma = pltpu.SemaphoreType.DMA
    return pl.pallas_call(
        functools.partial(march, sizes),
        out_shape=jax.ShapeDtypeStruct((steps, per, unknowns), jnp.float32),
        in_specs=[smem] * 5 + [vmem] * 7 + [pl.BlockSpec(memory_space=pl.ANY)],
        out_specs=vmem,
        scratch_shapes=[
            pltpu.VMEM(near_blocks.shape, near_blocks.dtype),
            pltpu.VMEM((3, side, side, span, 2, per, LANES), jnp.float32),
            pltpu.VMEM((side, side, span, quarters, LANES), jnp.float32),
            pltpu.VMEM((steps - 1, 3 * n_clus, 3, per, LANES), jnp.float32),
            pltpu.VMEM((steps, n_slab, quarters, LANES), jnp.float32),
            pltpu.VMEM((steps, n_slab, quarters, LANES), jnp.float32),
            pltpu.VMEM((n_slab, quarters, LANES), jnp.float32),
            pltpu.VMEM((2, per * slots, LANES), jnp.float32),
            pltpu.VMEM((per, unknowns, LANES), jnp.float32),
            pltpu.VMEM((quarters, LANES), jnp.float32),
            dma(()), dma((2, 2)), dma((2,)), dma((2,)), dma((2, 2)), dma((2,)), dma((2, side)), dma((2,)), dma((2,)),
            dma((steps - 1,)), dma((steps - 1,)), dma((steps - 1, 2)), dma((steps - 1, 2)),
            dma((steps,)), dma((steps,)),
        ],
        compiler_params=pltpu.CompilerParams(
            collective_id=0, has_side_effects=True, vmem_limit_bytes=48 * 1024 * 1024
        ),
    )(
        near_idx, near_cnt, near_lag, near_frac, code.reshape(-1),
        incident, history, rays, shift, inverses, far_weight, fresh_weight, near_blocks,
    )


def solution(mesh):
    split = ("slab", "clus")
    in_specs = (
        P(None, split, None),
        P(None, split, None),
        P(split, None, None, None),
        P(split, None),
        P(split),
        P(split, None),
        P(split, None),
        P(split, None, None),
        P(split, None, None),
        P(split, None),
        P(),
        P(),
        P(),
    )
    return jax.shard_map(local, mesh=mesh, in_specs=in_specs, out_specs=P(None, split, None), check_vma=False)
```

```python
import functools

import jax
import jax.numpy as jnp
from jax import lax
from jax.experimental import pallas as pl
from jax.experimental.pallas import tpu as pltpu
from jax.sharding import PartitionSpec as P

MESH = pl.DeviceIdType.MESH
LANES = 128
CHUNK = 32
SIDE = 4
FAR_FIRST = (
    (2, 2), (2, 1), (2, 3), (1, 2), (3, 2), (2, 0), (0, 2), (1, 1),
    (1, 3), (3, 1), (3, 3), (1, 0), (3, 0), (0, 1), (0, 3),
)
NT = (((1,), (1,)), ((), ()))
NN = (((1,), (0,)), ((), ()))


def dot(left, right, dims):
    return lax.dot_general(left, right, dims, preferred_element_type=jnp.float32)


def remote(src, dst, send, recv, device):
    return pltpu.make_async_remote_copy(
        src_ref=src, dst_ref=dst, send_sem=send, recv_sem=recv,
        device_id=device, device_id_type=MESH,
    )


def march(
    sizes,
    near_idx_hbm, near_cnt_hbm, near_lag_hbm, near_frac_hbm, far_idx_hbm, far_lag_hbm,
    incident_hbm, history_hbm, shift_hbm, near_hbm, rays_hbm, inverses_hbm, trans_hbm,
    out,
    near_idx, near_cnt, near_lag, near_frac, far_idx, far_lag, incident, history, shift,
    near, rays, inverses, trans, far_weight, fresh_weight, line, past, land, land_ray, part_out, part_in, early, blend, partial, incoming,
    small_sem, near_sem, rays_sem, inverses_sem, trans_sem, ray_send, ray_recv, ray_far_recv, cur_send, cur_recv, cur_far_recv, wide_send, wide_recv,
    one_send, one_recv, spec_send, spec_recv, fwd_send, fwd_recv, two_send, two_recv,
):
    steps, lags, n_slab, side, per, slots, unknowns, far_slots = sizes
    n_clus = side * side
    middle = lags // 2
    slab = lax.axis_index("slab")
    clus = lax.axis_index("clus")
    row, col = clus // side, lax.rem(clus, side)
    after = lax.rem(slab + 1, n_slab)
    before = lax.rem(slab + n_slab - 1, n_slab)
    tail = unknowns - LANES
    quarters = shift.shape[1] // LANES
    home = n_clus + clus
    early_half, late_half = pl.ds(0, middle), pl.ds(middle, lags - middle)

    barrier = pltpu.get_barrier_semaphore()

    def greet_plane(k, carry):
        pl.semaphore_signal(barrier, inc=1, device_id=(slab, lax.rem(clus + k, n_clus)), device_id_type=MESH)
        return carry

    def greet_column(k, carry):
        pl.semaphore_signal(barrier, inc=1, device_id=(lax.rem(slab + k, n_slab), clus), device_id_type=MESH)
        return carry

    small = [
        pltpu.make_async_copy(source, target, small_sem.at[n])
        for n, (source, target) in enumerate((
            (history_hbm, history), (shift_hbm, shift), (far_idx_hbm, far_idx), (far_lag_hbm, far_lag),
            (near_idx_hbm, near_idx), (near_lag_hbm, near_lag), (near_frac_hbm, near_frac),
            (near_cnt_hbm, near_cnt), (incident_hbm, incident),
        ))
    ]
    for fetch in small:
        fetch.start()
    fetch_rays = pltpu.make_async_copy(rays_hbm, rays, rays_sem)
    fetch_rays.start()
    lax.fori_loop(1, n_clus, greet_plane, 0)
    lax.fori_loop(1, n_slab, greet_column, 0)
    for group in range(n_slab):
        pltpu.make_async_copy(trans_hbm.at[group * n_clus + clus], trans.at[group], trans_sem).start()
    fetch_inverses = pltpu.make_async_copy(inverses_hbm, inverses, inverses_sem)
    fetch_inverses.start()
    fetch_near = pltpu.make_async_copy(near_hbm, near, near_sem)
    fetch_near.start()

    small[0].wait()
    line[1, row, col, pl.ds(0, lags), 0] = history[:, :, :LANES]
    line[1, row, col, pl.ds(0, lags), 1] = jnp.concatenate(
        [history[:, :, LANES:], jnp.zeros((lags, per, LANES - tail), jnp.float32)], axis=2)
    small[1].wait()
    fetch_rays.wait()
    spectra = jnp.zeros((lags, quarters * LANES), jnp.float32)
    for c in range(per):
        spectra += dot(history[:, c, :].astype(jnp.bfloat16), rays[c], NN) * shift[c:c + 1, :]
    for q in range(quarters):
        past[row, col, pl.ds(0, lags), q, :] = spectra[:, q * LANES:(q + 1) * LANES]
    pl.semaphore_wait(barrier, n_clus + n_slab - 2)

    def along_x(k):
        return (slab, row * side + lax.rem(col + k, side))

    def along_y(k):
        return (slab, lax.rem(row + k, side) * side + col)

    own_ray = [past.at[row, col, early_half], past.at[row, col, late_half]]
    own_cur = [line.at[1, row, col, early_half], line.at[1, row, col, late_half]]
    row_ray = [past.at[row, :, early_half], past.at[:, col, late_half]]

    def cur_strip(which, place):
        return line.at[1, place, :, early_half] if which == 0 else line.at[1, :, place, late_half]

    toward = [along_x, along_y]
    place = [row, col]

    def wide_start(which, spots):
        cut = early_half if which == 0 else late_half
        for side_of, device, slot in ((0, before, 2), (1, after, 0)):
            remote(line.at[(1,) + spots + (cut,)], line.at[(slot,) + spots + (cut,)],
                   wide_send.at[side_of], wide_recv.at[side_of], (device, clus)).start()

    for own, send, recv in ((own_cur, cur_send, cur_recv), (own_ray, ray_send, ray_recv)):
        for which in range(2):
            for k in (2, 1, 3):
                remote(own[which], own[which], send.at[0, which], recv.at[which], toward[which](k)).start()
        if own is own_cur:
            wide_start(0, (row, col))
            wide_start(1, (row, col))

    three_ray = [past.at[0, pl.ds(0, side - 1), early_half], past.at[0, pl.ds(0, side - 1), late_half]]
    three_cur = [line.at[1, 0, pl.ds(0, side - 1), early_half], line.at[1, 0, pl.ds(0, side - 1), late_half]]
    strips_ray = [past.at[pl.ds(0, side - 1), :, early_half], past.at[pl.ds(0, side - 1), :, late_half]]
    strips_cur = [line.at[1, pl.ds(0, side - 1), :, early_half], line.at[1, pl.ds(0, side - 1), :, late_half]]

    def waiter(piece, send, recv):
        return remote(piece, piece, send, recv, (slab, clus))

    for which in range(2):
        waiter(three_cur[which], cur_send.at[0, which], cur_recv.at[which]).wait_recv()
        strip = cur_strip(which, place[which])
        for k in (2, 1, 3):
            remote(strip, strip, cur_send.at[1, which], cur_far_recv.at[which, place[which]],
                   toward[1 - which](k)).start()
    for which in range(2):
        waiter(three_ray[which], ray_send.at[0, which], ray_recv.at[which]).wait_recv()
        for k in (2, 1, 3):
            remote(row_ray[which], row_ray[which], ray_send.at[1, which], ray_far_recv.at[which],
                   toward[1 - which](k)).start()
    for which in range(2):
        for k in (1, 3, 2):
            spots = (row, lax.rem(col + k, side)) if which == 0 else (lax.rem(row + k, side), col)
            wide_start(which, spots)

    small[2].wait()
    small[3].wait()
    pltpu.make_async_copy(trans_hbm.at[pl.ds(0, n_slab)], trans, trans_sem).wait()

    def weigh(target, carry):
        wide = trans[target].astype(jnp.float32)
        for q in range(quarters):
            far_weight[pl.ds(target * far_slots, far_slots), q, :] = wide[:, q * LANES:(q + 1) * LANES]
        tags, weights = [], []
        for slot in range(far_slots):
            entry = target * far_slots + slot
            group = far_idx[slot, target * n_clus + clus]
            lag = far_lag[slot, target * n_clus + clus]
            tag = jnp.where((lag == 1) & (lax.div(group, n_clus) == slab), lax.rem(group, n_clus), -1)
            tags.append(jnp.full((quarters, LANES), tag, jnp.int32))
            weights.append(far_weight[entry])
        for member in range(n_clus):
            total = jnp.zeros((quarters, LANES), jnp.float32)
            for slot in range(far_slots):
                total += jnp.where(tags[slot] == member, weights[slot], 0.0)
            fresh_weight[member, target] = total
        return carry

    lax.fori_loop(0, n_slab, weigh, 0)

    def whole_wide(which):
        piece = line.at[0, :, :, pl.ds(0, lags)]
        return waiter(piece, wide_send.at[which], wide_recv.at[which])

    def far_early(step):
        def one(target, carry):
            total = jnp.zeros((quarters, LANES), jnp.float32)
            for slot in range(far_slots):
                entry = target * far_slots + slot
                group = far_idx[slot, target * n_clus + clus]
                lag = far_lag[slot, target * n_clus + clus]
                member = lax.rem(group, n_clus)
                old = lag >= 2
                time = jnp.where(old, step + lags - lag, 0)
                mine = jnp.where(old & (lax.div(group, n_clus) == slab), 1.0, 0.0)
                total += (far_weight[entry] * mine) * past[lax.div(member, side), lax.rem(member, side), time]
            early[target] = total
            return carry

        lax.fori_loop(0, n_slab, one, 0)

    def far_send(step):
        totals = [
            jnp.concatenate([early[2 * p], early[2 * p + 1]], axis=0) for p in range(n_slab // 2)
        ]
        for member in range(n_clus):
            one = past[member // side, member % side, lags - 1 + step]
            both = jnp.concatenate([one, one], axis=0)
            for p in range(n_slab // 2):
                totals[p] += jnp.concatenate(
                    [fresh_weight[member, 2 * p], fresh_weight[member, 2 * p + 1]], axis=0) * both
        for p in range(n_slab // 2):
            part_out[step, 2 * p] = totals[p][:quarters]
            part_out[step, 2 * p + 1] = totals[p][quarters:]

        for k in sorted(range(1, n_slab), key=lambda k: -min(k, n_slab - k)):
            target = lax.rem(slab + k, n_slab)
            remote(part_out.at[step, target], part_in.at[step, slab],
                   two_send.at[step], two_recv.at[step], (target, clus)).start()
        part_in[step, slab] = part_out[step, slab]

    for k in (1, 3, 2):
        for which in range(2):
            spot = lax.rem(place[which] + k, side)
            waiter(cur_strip(which, spot), cur_send.at[1, which], cur_far_recv.at[which, spot]).wait_recv()
            wide_start(which, (spot, slice(None)) if which == 0 else (slice(None), spot))
    for which in range(2):
        waiter(strips_ray[which], ray_send.at[1, which], ray_far_recv.at[which]).wait_recv()
    far_early(0)
    far_send(0)

    whole_wide(0).wait_recv()
    whole_wide(1).wait_recv()
    fetch_inverses.wait()
    for n in range(4, 9):
        small[n].wait()
    fetch_near.wait()

    row_id = lax.broadcasted_iota(jnp.int32, (per, 1), 0)

    def whole_one(step):
        return waiter(land.at[step, pl.ds(0, n_clus - 1)], one_send.at[step], one_recv.at[step])

    def whole_spec(step):
        return waiter(land_ray.at[step, pl.ds(0, n_clus - 1)], spec_send.at[step], spec_recv.at[step])

    def whole_fwd(step, which):
        return waiter(land.at[step, pl.ds(0, n_clus)], fwd_send.at[step, which], fwd_recv.at[step, which])

    def whole_two(step):
        return waiter(part_in.at[step, pl.ds(0, n_slab - 1)], two_send.at[step], two_recv.at[step])

    def body(step, carry):
        @pl.when(step > 0)
        def _():
            last = step - 1
            for which, slot in ((0, 2), (1, 0)):
                whole_fwd(last, which).wait_recv()
                for k in range(n_clus):
                    line[slot, k // side, k % side, lags + last] = land[last, slot * n_clus + k]

        def blend_one(c, inner):
            for j in range(slots):
                entry = c * slots + j
                local_idx = jnp.clip(near_idx[c, j] - (slab - 1) * (n_clus * per), 0, 3 * n_clus * per - 1)
                device, sub = lax.div(local_idx, per), lax.rem(local_idx, per)
                spot = lax.rem(device, n_clus)
                index = (lax.div(device, n_clus), lax.div(spot, side), lax.rem(spot, side))
                time = step + lags - 1 - near_lag[c, j]
                live = j < near_cnt[c]
                now = jnp.where(live, 1.0 - near_frac[c, j], 0.0)
                old = jnp.where(live, near_frac[c, j], 0.0)
                for half in range(2):
                    mixed = (
                        now * line[index + (time + 1, half, pl.ds(sub, 1), slice(None))]
                        + old * line[index + (time, half, pl.ds(sub, 1), slice(None))]
                    )
                    blend[half, pl.ds(entry, 1), :] = mixed.astype(jnp.bfloat16).astype(jnp.float32)
            return inner

        lax.fori_loop(0, per, blend_one, 0)

        def near_one(c, inner):
            for first in range(0, unknowns, CHUNK):
                rows = min(CHUNK, unknowns - first)
                left = jnp.zeros((rows, LANES), jnp.float32)
                right = jnp.zeros((rows, tail), jnp.float32)
                for j in range(slots):
                    entry = c * slots + j
                    left += (near[c, j, pl.ds(first, rows), pl.ds(0, LANES)].astype(jnp.float32)
                             * blend[0, pl.ds(entry, 1), :])
                    right += (near[c, j, pl.ds(first, rows), pl.ds(LANES, tail)].astype(jnp.float32)
                              * blend[1, pl.ds(entry, 1), pl.ds(0, tail)])
                partial[c, pl.ds(first, rows), :] = left + jnp.concatenate(
                    [right, jnp.zeros((rows, LANES - tail), jnp.float32)], axis=1)
            return inner

        lax.fori_loop(0, per, near_one, 0)

        field = jnp.zeros((per, unknowns), jnp.float32)
        for c in range(per):
            pick = jnp.where(row_id == c, 1.0, 0.0) * jnp.ones((per, LANES), jnp.float32)
            pick = pick.astype(jnp.bfloat16)
            value = partial[c]
            high = value.astype(jnp.bfloat16)
            low = (value - high.astype(jnp.float32)).astype(jnp.bfloat16)
            field += dot(pick, high, NT) + dot(pick, low, NT)

        whole_two(step).wait_recv()
        incoming[...] = jnp.sum(part_in[step], axis=0)
        spread = jnp.concatenate(
            [shift[:, q * LANES:(q + 1) * LANES] * incoming[pl.ds(q, 1), :] for q in range(quarters)], axis=1)
        for c in range(per):
            field += dot(jnp.where(row_id == c, spread, 0.0).astype(jnp.bfloat16), rays[c], NT)
        right_side = (incident[step] - field).astype(jnp.bfloat16).astype(jnp.float32)
        current = jnp.zeros((per, unknowns), jnp.float32)
        for c in range(per):
            current += dot(jnp.where(row_id == c, right_side, 0.0).astype(jnp.bfloat16), inverses[c], NT)
        out[step] = current

        @pl.when(step < steps - 1)
        def _():
            land[step, home, 0] = current[:, :LANES]
            land[step, home, 1] = jnp.concatenate(
                [current[:, LANES:], jnp.zeros((per, LANES - tail), jnp.float32)], axis=1)
            for dy, dx in FAR_FIRST:
                piece = land.at[step, home]
                target = lax.rem(row + dy, side) * side + lax.rem(col + dx, side)
                remote(piece, piece, one_send.at[step], one_recv.at[step], (slab, target)).start()

            rounded = current.astype(jnp.bfloat16).astype(jnp.float32)
            values = jnp.zeros((per, quarters * LANES), jnp.float32)
            for c in range(per):
                values += dot(jnp.where(row_id == c, rounded, 0.0).astype(jnp.bfloat16), rays[c], NN)
            spectrum = jnp.sum(values * shift[...], axis=0, keepdims=True)
            for q in range(quarters):
                land_ray[step, clus, pl.ds(q, 1), :] = spectrum[:, q * LANES:(q + 1) * LANES]

            for dy, dx in FAR_FIRST:
                piece = land_ray.at[step, clus]
                target = lax.rem(row + dy, side) * side + lax.rem(col + dx, side)
                remote(piece, piece, spec_send.at[step], spec_recv.at[step], (slab, target)).start()

            far_early(step + 1)
            whole_one(step).wait_recv()
            piece = land.at[step, pl.ds(n_clus, n_clus)]
            remote(piece, land.at[step, pl.ds(2 * n_clus, n_clus)],
                   fwd_send.at[step, 0], fwd_recv.at[step, 0], (before, clus)).start()
            remote(piece, land.at[step, pl.ds(0, n_clus)],
                   fwd_send.at[step, 1], fwd_recv.at[step, 1], (after, clus)).start()
            whole_spec(step).wait_recv()
            for k in range(n_clus):
                past[k // side, k % side, lags + step] = land_ray[step, k]
            far_send(step + 1)
            for k in range(n_clus):
                line[1, k // side, k % side, lags + step] = land[step, n_clus + k]

        return carry

    lax.fori_loop(0, steps, body, 0)

    for which in range(2):
        waiter(three_ray[which], ray_send.at[0, which], ray_recv.at[which]).wait_send()
        waiter(three_cur[which], cur_send.at[0, which], cur_recv.at[which]).wait_send()
        waiter(strips_ray[which], ray_send.at[1, which], ray_recv.at[which]).wait_send()
        waiter(strips_cur[which], cur_send.at[1, which], cur_recv.at[which]).wait_send()
        whole_wide(which).wait_send()

    def finish(step, carry):
        whole_two(step).wait_send()

        @pl.when(step < steps - 1)
        def _():
            whole_one(step).wait_send()
            whole_spec(step).wait_send()
            whole_fwd(step, 0).wait_send()
            whole_fwd(step, 1).wait_send()

        return carry

    lax.fori_loop(0, steps, finish, 0)


def local(
    incident, history, near_blocks, near_idx, near_cnt, near_lag, near_frac,
    inverses, rays, shift, far_idx, far_lag, trans,
):
    lags, per, unknowns = history.shape
    steps = incident.shape[0]
    slots = near_idx.shape[1]
    far_slots = far_idx.shape[1]
    n_slab = lax.axis_size("slab")
    n_clus = lax.axis_size("clus")
    side = SIDE
    span = lags + steps
    quarters = rays.shape[1] // LANES
    sizes = (steps, lags, n_slab, side, per, slots, unknowns, far_slots)
    vmem = pl.BlockSpec(memory_space=pltpu.VMEM)
    dma = pltpu.SemaphoreType.DMA
    return pl.pallas_call(
        functools.partial(march, sizes),
        out_shape=jax.ShapeDtypeStruct((steps, per, unknowns), jnp.float32),
        in_specs=[pl.BlockSpec(memory_space=pltpu.HBM)] * 13,
        out_specs=vmem,
        scratch_shapes=[
            pltpu.SMEM(near_idx.shape, jnp.int32),
            pltpu.SMEM(near_cnt.shape, jnp.int32),
            pltpu.SMEM(near_lag.shape, jnp.int32),
            pltpu.SMEM(near_frac.shape, jnp.float32),
            pltpu.SMEM(far_idx.shape[::-1], jnp.int32),
            pltpu.SMEM(far_lag.shape[::-1], jnp.int32),
            pltpu.VMEM(incident.shape, jnp.float32),
            pltpu.VMEM(history.shape, jnp.float32),
            pltpu.VMEM(shift.shape, jnp.float32),
            pltpu.VMEM(near_blocks.shape, near_blocks.dtype),
            pltpu.VMEM((rays.shape[0],) + rays.shape[:0:-1], rays.dtype),
            pltpu.VMEM(inverses.shape, inverses.dtype),
            pltpu.VMEM((n_slab,) + trans.shape[1:], trans.dtype),
            pltpu.VMEM((n_slab * far_slots, quarters, LANES), jnp.float32),
            pltpu.VMEM((n_clus, n_slab, quarters, LANES), jnp.float32),
            pltpu.VMEM((3, side, side, span, 2, per, LANES), jnp.float32),
            pltpu.VMEM((side, side, span, quarters, LANES), jnp.float32),
            pltpu.VMEM((steps - 1, 3 * n_clus, 2, per, LANES), jnp.float32),
            pltpu.VMEM((steps - 1, n_clus, quarters, LANES), jnp.float32),
            pltpu.VMEM((steps, n_slab, quarters, LANES), jnp.float32),
            pltpu.VMEM((steps, n_slab, quarters, LANES), jnp.float32),
            pltpu.VMEM((n_slab, quarters, LANES), jnp.float32),
            pltpu.VMEM((2, per * slots, LANES), jnp.float32),
            pltpu.VMEM((per, unknowns, LANES), jnp.float32),
            pltpu.VMEM((quarters, LANES), jnp.float32),
            dma((9,)), dma(()), dma(()), dma(()), dma(()), dma((2, 2)), dma((2,)), dma((2,)), dma((2, 2)), dma((2,)), dma((2, side)), dma((2,)), dma((2,)),
            dma((steps - 1,)), dma((steps - 1,)), dma((steps - 1,)), dma((steps - 1,)), dma((steps - 1, 2)), dma((steps - 1, 2)),
            dma((steps,)), dma((steps,)),
        ],
        compiler_params=pltpu.CompilerParams(
            collective_id=0, has_side_effects=True, vmem_limit_bytes=63 * 1024 * 1024
        ),
    )(
        near_idx, near_cnt, near_lag, near_frac, far_idx.T, far_lag.T,
        incident, history, shift, near_blocks, jnp.swapaxes(rays, 1, 2), inverses, trans,
    )


def solution(mesh):
    split = ("slab", "clus")
    in_specs = (
        P(None, split, None),
        P(None, split, None),
        P(split, None, None, None),
        P(split, None),
        P(split),
        P(split, None),
        P(split, None),
        P(split, None, None),
        P(split, None, None),
        P(split, None),
        P(),
        P(),
        P(),
    )
    return jax.shard_map(local, mesh=mesh, in_specs=in_specs, out_specs=P(None, split, None), check_vma=False)
```

```python
import functools

import jax
import jax.numpy as jnp
from jax import lax
from jax.experimental import pallas as pl
from jax.experimental.pallas import tpu as pltpu
from jax.sharding import PartitionSpec as P

MESH = pl.DeviceIdType.MESH
LANES = 128
CHUNK = 32
SIDE = 4
FAR_FIRST = (
    (2, 2), (2, 1), (2, 3), (1, 2), (3, 2), (2, 0), (0, 2), (1, 1),
    (1, 3), (3, 1), (3, 3), (1, 0), (3, 0), (0, 1), (0, 3),
)
NT = (((1,), (1,)), ((), ()))
NN = (((1,), (0,)), ((), ()))


def dot(left, right, dims):
    return lax.dot_general(left, right, dims, preferred_element_type=jnp.float32)


def remote(src, dst, send, recv, device):
    return pltpu.make_async_remote_copy(
        src_ref=src, dst_ref=dst, send_sem=send, recv_sem=recv,
        device_id=device, device_id_type=MESH,
    )


def march(
    sizes,
    near_idx_hbm, near_cnt_hbm, near_lag_hbm, near_frac_hbm, far_idx_hbm, far_lag_hbm,
    incident_hbm, history_hbm, shift_hbm, near_hbm, rays_hbm, inverses_hbm, trans_hbm,
    out,
    near_idx, near_cnt, near_lag, near_frac, near_at, near_mix, far_at, far_mine, far_idx, far_lag, incident, history, shift,
    near, rays, rays_back, inverses, trans, far_weight, fresh_weight, line, past, land, land_ray, part_out, part_in, early, blend, partial, incoming,
    small_sem, near_sem, rays_sem, inverses_sem, trans_sem, ray_send, ray_recv, ray_far_recv, cur_send, cur_recv, cur_far_recv, wide_send, wide_recv,
    one_send, one_recv, spec_send, spec_recv, fwd_send, fwd_recv, two_send, two_recv,
):
    steps, lags, n_slab, side, per, slots, unknowns, far_slots = sizes
    n_clus = side * side
    middle = lags // 2
    slab = lax.axis_index("slab")
    clus = lax.axis_index("clus")
    row, col = clus // side, lax.rem(clus, side)
    after = lax.rem(slab + 1, n_slab)
    before = lax.rem(slab + n_slab - 1, n_slab)
    tail = unknowns - LANES
    quarters = shift.shape[1] // LANES
    home = n_clus + clus
    early_half, late_half = pl.ds(0, middle), pl.ds(middle, lags - middle)

    barrier = pltpu.get_barrier_semaphore()

    def greet_plane(k, carry):
        pl.semaphore_signal(barrier, inc=1, device_id=(slab, lax.rem(clus + k, n_clus)), device_id_type=MESH)
        return carry

    def greet_column(k, carry):
        pl.semaphore_signal(barrier, inc=1, device_id=(lax.rem(slab + k, n_slab), clus), device_id_type=MESH)
        return carry

    small = [
        pltpu.make_async_copy(source, target, small_sem.at[n])
        for n, (source, target) in enumerate((
            (history_hbm, history), (shift_hbm, shift), (far_idx_hbm, far_idx), (far_lag_hbm, far_lag),
            (near_idx_hbm, near_idx), (near_lag_hbm, near_lag), (near_frac_hbm, near_frac),
            (near_cnt_hbm, near_cnt), (incident_hbm, incident),
        ))
    ]
    for fetch in small:
        fetch.start()
    fetch_rays = pltpu.make_async_copy(rays_hbm, rays, rays_sem)
    fetch_rays.start()
    lax.fori_loop(1, n_clus, greet_plane, 0)
    lax.fori_loop(1, n_slab, greet_column, 0)
    for group in range(n_slab):
        pltpu.make_async_copy(trans_hbm.at[group * n_clus + clus], trans.at[group], trans_sem).start()
    fetch_inverses = pltpu.make_async_copy(inverses_hbm, inverses, inverses_sem)
    fetch_inverses.start()
    fetch_near = pltpu.make_async_copy(near_hbm, near, near_sem)
    fetch_near.start()

    small[0].wait()
    line[1, row, col, pl.ds(0, lags), 0] = history[:, :, :LANES]
    line[1, row, col, pl.ds(0, lags), 1] = jnp.concatenate(
        [history[:, :, LANES:], jnp.zeros((lags, per, LANES - tail), jnp.float32)], axis=2)
    small[1].wait()
    fetch_rays.wait()
    spectra = jnp.zeros((lags, quarters * LANES), jnp.float32)
    for c in range(per):
        spectra += dot(history[:, c, :].astype(jnp.bfloat16), rays[c], NN) * shift[c:c + 1, :]
    for q in range(quarters):
        past[row, col, pl.ds(0, lags), q, :] = spectra[:, q * LANES:(q + 1) * LANES]
    pl.semaphore_wait(barrier, n_clus + n_slab - 2)

    def along_x(k):
        return (slab, row * side + lax.rem(col + k, side))

    def along_y(k):
        return (slab, lax.rem(row + k, side) * side + col)

    own_ray = [past.at[row, col, early_half], past.at[row, col, late_half]]
    own_cur = [line.at[1, row, col, early_half], line.at[1, row, col, late_half]]
    row_ray = [past.at[row, :, early_half], past.at[:, col, late_half]]

    def cur_strip(which, place):
        return line.at[1, place, :, early_half] if which == 0 else line.at[1, :, place, late_half]

    toward = [along_x, along_y]
    place = [row, col]

    def wide_start(which, spots):
        cut = early_half if which == 0 else late_half
        for side_of, device, slot in ((0, before, 2), (1, after, 0)):
            remote(line.at[(1,) + spots + (cut,)], line.at[(slot,) + spots + (cut,)],
                   wide_send.at[side_of], wide_recv.at[side_of], (device, clus)).start()

    for own, send, recv in ((own_ray, ray_send, ray_recv), (own_cur, cur_send, cur_recv)):
        for which in range(2):
            for k in (2, 1, 3):
                remote(own[which], own[which], send.at[0, which], recv.at[which], toward[which](k)).start()
        if own is own_cur:
            wide_start(0, (row, col))
            wide_start(1, (row, col))

    three_ray = [past.at[0, pl.ds(0, side - 1), early_half], past.at[0, pl.ds(0, side - 1), late_half]]
    three_cur = [line.at[1, 0, pl.ds(0, side - 1), early_half], line.at[1, 0, pl.ds(0, side - 1), late_half]]
    strips_ray = [past.at[pl.ds(0, side - 1), :, early_half], past.at[pl.ds(0, side - 1), :, late_half]]
    strips_cur = [line.at[1, pl.ds(0, side - 1), :, early_half], line.at[1, pl.ds(0, side - 1), :, late_half]]

    def waiter(piece, send, recv):
        return remote(piece, piece, send, recv, (slab, clus))

    for which in range(2):
        waiter(three_ray[which], ray_send.at[0, which], ray_recv.at[which]).wait_recv()
        for k in (2, 1, 3):
            remote(row_ray[which], row_ray[which], ray_send.at[1, which], ray_far_recv.at[which],
                   toward[1 - which](k)).start()
    for which in range(2):
        waiter(three_cur[which], cur_send.at[0, which], cur_recv.at[which]).wait_recv()
        strip = cur_strip(which, place[which])
        for k in (2, 1, 3):
            remote(strip, strip, cur_send.at[1, which], cur_far_recv.at[which, place[which]],
                   toward[1 - which](k)).start()
    for which in range(2):
        for k in (1, 3, 2):
            spots = (row, lax.rem(col + k, side)) if which == 0 else (lax.rem(row + k, side), col)
            wide_start(which, spots)

    small[2].wait()
    small[3].wait()
    pltpu.make_async_copy(trans_hbm.at[pl.ds(0, n_slab)], trans, trans_sem).wait()

    def weigh(target, carry):
        wide = trans[target].astype(jnp.float32)
        for q in range(quarters):
            far_weight[pl.ds(target * far_slots, far_slots), q, :] = wide[:, q * LANES:(q + 1) * LANES]
        tags, weights = [], []
        for slot in range(far_slots):
            entry = target * far_slots + slot
            group = far_idx[slot, target * n_clus + clus]
            lag = far_lag[slot, target * n_clus + clus]
            old = lag >= 2
            member = lax.rem(group, n_clus)
            far_at[0, entry] = lax.div(member, side)
            far_at[1, entry] = lax.rem(member, side)
            far_at[2, entry] = jnp.where(old, lags - lag, 0)
            far_mine[entry] = jnp.where(old & (lax.div(group, n_clus) == slab), 1.0, 0.0)
            tag = jnp.where((lag == 1) & (lax.div(group, n_clus) == slab), lax.rem(group, n_clus), -1)
            tags.append(jnp.full((quarters, LANES), tag, jnp.int32))
            weights.append(far_weight[entry])
        for member in range(n_clus):
            total = jnp.zeros((quarters, LANES), jnp.float32)
            for slot in range(far_slots):
                total += jnp.where(tags[slot] == member, weights[slot], 0.0)
            fresh_weight[member, target] = total
        return carry

    lax.fori_loop(0, n_slab, weigh, 0)

    def turn(c, carry):
        for q in range(quarters):
            wide = rays[c, :, pl.ds(q * LANES, LANES)].astype(jnp.float32)
            rays_back[c, pl.ds(q * LANES, LANES), :] = wide.T.astype(jnp.bfloat16)
        return carry

    lax.fori_loop(0, per, turn, 0)

    for n in range(4, 9):
        small[n].wait()

    def locate(c, carry):
        for j in range(slots):
            entry = c * slots + j
            local_idx = jnp.clip(near_idx[c, j] - (slab - 1) * (n_clus * per), 0, 3 * n_clus * per - 1)
            device = lax.div(local_idx, per)
            spot = lax.rem(device, n_clus)
            near_at[0, entry] = lax.div(device, n_clus)
            near_at[1, entry] = lax.div(spot, side)
            near_at[2, entry] = lax.rem(spot, side)
            near_at[3, entry] = lax.rem(local_idx, per)
            near_at[4, entry] = lags - 1 - near_lag[c, j]
            live = j < near_cnt[c]
            near_mix[0, entry] = jnp.where(live, 1.0 - near_frac[c, j], 0.0)
            near_mix[1, entry] = jnp.where(live, near_frac[c, j], 0.0)
        return carry

    lax.fori_loop(0, per, locate, 0)

    def whole_wide(which):
        piece = line.at[0, :, :, pl.ds(0, lags)]
        return waiter(piece, wide_send.at[which], wide_recv.at[which])

    def far_early(step):
        def one(target, carry):
            total = jnp.zeros((quarters, LANES), jnp.float32)
            for slot in range(far_slots):
                entry = target * far_slots + slot
                time = step + far_at[2, entry]
                total += (far_weight[entry] * far_mine[entry]) * past[far_at[0, entry], far_at[1, entry], time]
            early[target] = total
            return carry

        lax.fori_loop(0, n_slab, one, 0)

    def far_send(step):
        totals = [
            jnp.concatenate([early[2 * p], early[2 * p + 1]], axis=0) for p in range(n_slab // 2)
        ]
        for member in range(n_clus):
            one = past[member // side, member % side, lags - 1 + step]
            both = jnp.concatenate([one, one], axis=0)
            for p in range(n_slab // 2):
                totals[p] += jnp.concatenate(
                    [fresh_weight[member, 2 * p], fresh_weight[member, 2 * p + 1]], axis=0) * both
        for p in range(n_slab // 2):
            part_out[step, 2 * p] = totals[p][:quarters]
            part_out[step, 2 * p + 1] = totals[p][quarters:]

        for k in sorted(range(1, n_slab), key=lambda k: -min(k, n_slab - k)):
            target = lax.rem(slab + k, n_slab)
            remote(part_out.at[step, target], part_in.at[step, slab],
                   two_send.at[step], two_recv.at[step], (target, clus)).start()
        part_in[step, slab] = part_out[step, slab]

    for which in range(2):
        waiter(strips_ray[which], ray_send.at[1, which], ray_far_recv.at[which]).wait_recv()
    far_early(0)
    far_send(0)
    for k in (1, 3, 2):
        for which in range(2):
            spot = lax.rem(place[which] + k, side)
            waiter(cur_strip(which, spot), cur_send.at[1, which], cur_far_recv.at[which, spot]).wait_recv()
            wide_start(which, (spot, slice(None)) if which == 0 else (slice(None), spot))

    whole_wide(0).wait_recv()
    whole_wide(1).wait_recv()
    fetch_inverses.wait()
    fetch_near.wait()

    row_id = lax.broadcasted_iota(jnp.int32, (per, 1), 0)

    def whole_one(step):
        return waiter(land.at[step, pl.ds(0, n_clus - 1)], one_send.at[step], one_recv.at[step])

    def whole_spec(step):
        return waiter(land_ray.at[step, pl.ds(0, n_clus - 1)], spec_send.at[step], spec_recv.at[step])

    def whole_fwd(step, which):
        return waiter(land.at[step, pl.ds(0, n_clus)], fwd_send.at[step, which], fwd_recv.at[step, which])

    def whole_two(step):
        return waiter(part_in.at[step, pl.ds(0, n_slab - 1)], two_send.at[step], two_recv.at[step])

    def body(step, carry):
        @pl.when(step > 0)
        def _():
            last = step - 1
            for which, slot in ((0, 2), (1, 0)):
                whole_fwd(last, which).wait_recv()
                for k in range(n_clus):
                    line[slot, k // side, k % side, lags + last] = land[last, slot * n_clus + k]

        def blend_one(c, inner):
            for j in range(slots):
                entry = c * slots + j
                index = (near_at[0, entry], near_at[1, entry], near_at[2, entry])
                sub = near_at[3, entry]
                time = step + near_at[4, entry]
                now, old = near_mix[0, entry], near_mix[1, entry]
                for half in range(2):
                    mixed = (
                        now * line[index + (time + 1, half, pl.ds(sub, 1), slice(None))]
                        + old * line[index + (time, half, pl.ds(sub, 1), slice(None))]
                    )
                    blend[half, pl.ds(entry, 1), :] = mixed.astype(jnp.bfloat16).astype(jnp.float32)
            return inner

        lax.fori_loop(0, per, blend_one, 0)

        def near_one(c, inner):
            for first in range(0, unknowns, CHUNK):
                rows = min(CHUNK, unknowns - first)
                left = jnp.zeros((rows, LANES), jnp.float32)
                right = jnp.zeros((rows, tail), jnp.float32)
                for j in range(slots):
                    entry = c * slots + j
                    left += (near[c, j, pl.ds(first, rows), pl.ds(0, LANES)].astype(jnp.float32)
                             * blend[0, pl.ds(entry, 1), :])
                    right += (near[c, j, pl.ds(first, rows), pl.ds(LANES, tail)].astype(jnp.float32)
                              * blend[1, pl.ds(entry, 1), pl.ds(0, tail)])
                partial[c, pl.ds(first, rows), :] = left + jnp.concatenate(
                    [right, jnp.zeros((rows, LANES - tail), jnp.float32)], axis=1)
            return inner

        lax.fori_loop(0, per, near_one, 0)

        field = jnp.zeros((per, unknowns), jnp.float32)
        for c in range(per):
            pick = jnp.where(row_id == c, 1.0, 0.0) * jnp.ones((per, 2 * LANES), jnp.float32)
            pick = pick.astype(jnp.bfloat16)
            value = partial[c]
            high = value.astype(jnp.bfloat16)
            low = (value - high.astype(jnp.float32)).astype(jnp.bfloat16)
            field += dot(pick, jnp.concatenate([high, low], axis=1), NT)

        whole_two(step).wait_recv()
        incoming[...] = jnp.sum(part_in[step], axis=0)
        spread = jnp.concatenate(
            [shift[:, q * LANES:(q + 1) * LANES] * incoming[pl.ds(q, 1), :] for q in range(quarters)], axis=1)
        for c in range(per):
            field += dot(jnp.where(row_id == c, spread, 0.0).astype(jnp.bfloat16), rays_back[c], NN)
        right_side = (incident[step] - field).astype(jnp.bfloat16).astype(jnp.float32)
        current = jnp.zeros((per, unknowns), jnp.float32)
        for c in range(per):
            current += dot(jnp.where(row_id == c, right_side, 0.0).astype(jnp.bfloat16), inverses[c], NT)
        out[step] = current

        @pl.when(step < steps - 1)
        def _():
            land[step, home, 0] = current[:, :LANES]
            land[step, home, 1] = jnp.concatenate(
                [current[:, LANES:], jnp.zeros((per, LANES - tail), jnp.float32)], axis=1)
            for dy, dx in FAR_FIRST:
                piece = land.at[step, home]
                target = lax.rem(row + dy, side) * side + lax.rem(col + dx, side)
                remote(piece, piece, one_send.at[step], one_recv.at[step], (slab, target)).start()

            rounded = current.astype(jnp.bfloat16).astype(jnp.float32)
            values = jnp.zeros((per, quarters * LANES), jnp.float32)
            for c in range(per):
                values += dot(jnp.where(row_id == c, rounded, 0.0).astype(jnp.bfloat16), rays[c], NN)
            spectrum = jnp.sum(values * shift[...], axis=0, keepdims=True)
            for q in range(quarters):
                land_ray[step, clus, pl.ds(q, 1), :] = spectrum[:, q * LANES:(q + 1) * LANES]

            for dy, dx in FAR_FIRST:
                piece = land_ray.at[step, clus]
                target = lax.rem(row + dy, side) * side + lax.rem(col + dx, side)
                remote(piece, piece, spec_send.at[step], spec_recv.at[step], (slab, target)).start()

            far_early(step + 1)
            whole_one(step).wait_recv()
            piece = land.at[step, pl.ds(n_clus, n_clus)]
            remote(piece, land.at[step, pl.ds(2 * n_clus, n_clus)],
                   fwd_send.at[step, 0], fwd_recv.at[step, 0], (before, clus)).start()
            remote(piece, land.at[step, pl.ds(0, n_clus)],
                   fwd_send.at[step, 1], fwd_recv.at[step, 1], (after, clus)).start()
            whole_spec(step).wait_recv()
            for k in range(n_clus):
                past[k // side, k % side, lags + step] = land_ray[step, k]
            far_send(step + 1)
            for k in range(n_clus):
                line[1, k // side, k % side, lags + step] = land[step, n_clus + k]

        return carry

    lax.fori_loop(0, steps, body, 0)

    for which in range(2):
        waiter(three_ray[which], ray_send.at[0, which], ray_recv.at[which]).wait_send()
        waiter(three_cur[which], cur_send.at[0, which], cur_recv.at[which]).wait_send()
        waiter(strips_ray[which], ray_send.at[1, which], ray_recv.at[which]).wait_send()
        waiter(strips_cur[which], cur_send.at[1, which], cur_recv.at[which]).wait_send()
        whole_wide(which).wait_send()

    def finish(step, carry):
        whole_two(step).wait_send()

        @pl.when(step < steps - 1)
        def _():
            whole_one(step).wait_send()
            whole_spec(step).wait_send()
            whole_fwd(step, 0).wait_send()
            whole_fwd(step, 1).wait_send()

        return carry

    lax.fori_loop(0, steps, finish, 0)


def local(
    incident, history, near_blocks, near_idx, near_cnt, near_lag, near_frac,
    inverses, rays, shift, far_idx, far_lag, trans,
):
    lags, per, unknowns = history.shape
    steps = incident.shape[0]
    slots = near_idx.shape[1]
    far_slots = far_idx.shape[1]
    n_slab = lax.axis_size("slab")
    n_clus = lax.axis_size("clus")
    side = SIDE
    span = lags + steps
    quarters = rays.shape[1] // LANES
    sizes = (steps, lags, n_slab, side, per, slots, unknowns, far_slots)
    vmem = pl.BlockSpec(memory_space=pltpu.VMEM)
    dma = pltpu.SemaphoreType.DMA
    return pl.pallas_call(
        functools.partial(march, sizes),
        out_shape=jax.ShapeDtypeStruct((steps, per, unknowns), jnp.float32),
        in_specs=[pl.BlockSpec(memory_space=pltpu.HBM)] * 13,
        out_specs=vmem,
        scratch_shapes=[
            pltpu.SMEM(near_idx.shape, jnp.int32),
            pltpu.SMEM(near_cnt.shape, jnp.int32),
            pltpu.SMEM(near_lag.shape, jnp.int32),
            pltpu.SMEM(near_frac.shape, jnp.float32),
            pltpu.SMEM((5, per * slots), jnp.int32),
            pltpu.SMEM((2, per * slots), jnp.float32),
            pltpu.SMEM((3, n_slab * far_slots), jnp.int32),
            pltpu.SMEM((n_slab * far_slots,), jnp.float32),
            pltpu.SMEM(far_idx.shape[::-1], jnp.int32),
            pltpu.SMEM(far_lag.shape[::-1], jnp.int32),
            pltpu.VMEM(incident.shape, jnp.float32),
            pltpu.VMEM(history.shape, jnp.float32),
            pltpu.VMEM(shift.shape, jnp.float32),
            pltpu.VMEM(near_blocks.shape, near_blocks.dtype),
            pltpu.VMEM((rays.shape[0],) + rays.shape[:0:-1], rays.dtype),
            pltpu.VMEM(rays.shape, rays.dtype),
            pltpu.VMEM(inverses.shape, inverses.dtype),
            pltpu.VMEM((n_slab,) + trans.shape[1:], trans.dtype),
            pltpu.VMEM((n_slab * far_slots, quarters, LANES), jnp.float32),
            pltpu.VMEM((n_clus, n_slab, quarters, LANES), jnp.float32),
            pltpu.VMEM((3, side, side, span, 2, per, LANES), jnp.float32),
            pltpu.VMEM((side, side, span, quarters, LANES), jnp.float32),
            pltpu.VMEM((steps - 1, 3 * n_clus, 2, per, LANES), jnp.float32),
            pltpu.VMEM((steps - 1, n_clus, quarters, LANES), jnp.float32),
            pltpu.VMEM((steps, n_slab, quarters, LANES), jnp.float32),
            pltpu.VMEM((steps, n_slab, quarters, LANES), jnp.float32),
            pltpu.VMEM((n_slab, quarters, LANES), jnp.float32),
            pltpu.VMEM((2, per * slots, LANES), jnp.float32),
            pltpu.VMEM((per, unknowns, LANES), jnp.float32),
            pltpu.VMEM((quarters, LANES), jnp.float32),
            dma((9,)), dma(()), dma(()), dma(()), dma(()), dma((2, 2)), dma((2,)), dma((2,)), dma((2, 2)), dma((2,)), dma((2, side)), dma((2,)), dma((2,)),
            dma((steps - 1,)), dma((steps - 1,)), dma((steps - 1,)), dma((steps - 1,)), dma((steps - 1, 2)), dma((steps - 1, 2)),
            dma((steps,)), dma((steps,)),
        ],
        compiler_params=pltpu.CompilerParams(
            collective_id=0, has_side_effects=True, vmem_limit_bytes=63 * 1024 * 1024
        ),
    )(
        near_idx, near_cnt, near_lag, near_frac, far_idx.T, far_lag.T,
        incident, history, shift, near_blocks, jnp.swapaxes(rays, 1, 2), inverses, trans,
    )


def solution(mesh):
    split = ("slab", "clus")
    in_specs = (
        P(None, split, None),
        P(None, split, None),
        P(split, None, None, None),
        P(split, None),
        P(split),
        P(split, None),
        P(split, None),
        P(split, None, None),
        P(split, None, None),
        P(split, None),
        P(),
        P(),
        P(),
    )
    return jax.shard_map(local, mesh=mesh, in_specs=in_specs, out_specs=P(None, split, None), check_vma=False)
```

```python
import functools

import jax
import jax.numpy as jnp
from jax import lax
from jax.experimental import pallas as pl
from jax.experimental.pallas import tpu as pltpu
from jax.sharding import PartitionSpec as P

MESH = pl.DeviceIdType.MESH
LANES = 128
CHUNK = 32
SIDE = 4
FAR_FIRST = (
    (2, 2), (2, 1), (2, 3), (1, 2), (3, 2), (2, 0), (0, 2), (1, 1),
    (1, 3), (3, 1), (3, 3), (1, 0), (3, 0), (0, 1), (0, 3),
)
NT = (((1,), (1,)), ((), ()))
NN = (((1,), (0,)), ((), ()))


def dot(left, right, dims):
    return lax.dot_general(left, right, dims, preferred_element_type=jnp.float32)


def remote(src, dst, send, recv, device):
    return pltpu.make_async_remote_copy(
        src_ref=src, dst_ref=dst, send_sem=send, recv_sem=recv,
        device_id=device, device_id_type=MESH,
    )


def march(
    sizes,
    near_idx_hbm, near_cnt_hbm, near_lag_hbm, near_frac_hbm, far_idx_hbm, far_lag_hbm,
    incident_hbm, history_hbm, shift_hbm, near_hbm, rays_hbm, inverses_hbm, trans_hbm,
    out,
    near_idx, near_cnt, near_lag, near_frac, near_at, near_mix, far_at, far_mine, far_idx, far_lag, incident, history, shift,
    near, rays, rays_back, inverses, trans, far_weight, fresh_weight, line, past, land, land_ray, part_out, part_in, early, blend, partial, incoming,
    small_sem, near_sem, rays_sem, inverses_sem, trans_sem, ray_send, ray_recv, ray_far_recv, cur_send, cur_recv, cur_far_recv, wide_send, wide_recv,
    one_send, one_recv, spec_send, spec_recv, fwd_send, fwd_recv, two_send, two_recv,
):
    steps, lags, n_slab, side, per, slots, unknowns, far_slots = sizes
    n_clus = side * side
    middle = lags // 2
    slab = lax.axis_index("slab")
    clus = lax.axis_index("clus")
    row, col = clus // side, lax.rem(clus, side)
    after = lax.rem(slab + 1, n_slab)
    before = lax.rem(slab + n_slab - 1, n_slab)
    tail = unknowns - LANES
    quarters = shift.shape[1] // LANES
    home = n_clus + clus
    early_half, late_half = pl.ds(0, middle), pl.ds(middle, lags - middle)

    barrier = pltpu.get_barrier_semaphore()

    def greet_plane(k, carry):
        pl.semaphore_signal(barrier, inc=1, device_id=(slab, lax.rem(clus + k, n_clus)), device_id_type=MESH)
        return carry

    def greet_column(k, carry):
        pl.semaphore_signal(barrier, inc=1, device_id=(lax.rem(slab + k, n_slab), clus), device_id_type=MESH)
        return carry

    lax.fori_loop(1, n_clus, greet_plane, 0)
    lax.fori_loop(1, n_slab, greet_column, 0)
    small = [
        pltpu.make_async_copy(source, target, small_sem.at[n])
        for n, (source, target) in enumerate((
            (history_hbm, history), (shift_hbm, shift), (far_idx_hbm, far_idx), (far_lag_hbm, far_lag),
            (near_idx_hbm, near_idx), (near_lag_hbm, near_lag), (near_frac_hbm, near_frac),
            (near_cnt_hbm, near_cnt), (incident_hbm, incident),
        ))
    ]
    for fetch in small:
        fetch.start()
    fetch_rays = pltpu.make_async_copy(rays_hbm, rays, rays_sem)
    fetch_rays.start()
    for group in range(n_slab):
        pltpu.make_async_copy(trans_hbm.at[group * n_clus + clus], trans.at[group], trans_sem).start()
    fetch_inverses = pltpu.make_async_copy(inverses_hbm, inverses, inverses_sem)
    fetch_inverses.start()
    fetch_near = pltpu.make_async_copy(near_hbm, near, near_sem)
    fetch_near.start()

    small[0].wait()
    line[1, row, col, pl.ds(0, lags), 0] = history[:, :, :LANES]
    line[1, row, col, pl.ds(0, lags), 1] = jnp.concatenate(
        [history[:, :, LANES:], jnp.zeros((lags, per, LANES - tail), jnp.float32)], axis=2)
    small[1].wait()
    fetch_rays.wait()
    spectra = jnp.zeros((lags, quarters * LANES), jnp.float32)
    for c in range(per):
        spectra += dot(history[:, c, :].astype(jnp.bfloat16), rays[c], NN) * shift[c:c + 1, :]
    for q in range(quarters):
        past[row, col, pl.ds(0, lags), q, :] = spectra[:, q * LANES:(q + 1) * LANES]
    pl.semaphore_wait(barrier, n_clus + n_slab - 2)

    def along_x(k):
        return (slab, row * side + lax.rem(col + k, side))

    def along_y(k):
        return (slab, lax.rem(row + k, side) * side + col)

    own_ray = [past.at[row, col, early_half], past.at[row, col, late_half]]
    own_cur = [line.at[1, row, col, early_half], line.at[1, row, col, late_half]]
    row_ray = [past.at[row, :, early_half], past.at[:, col, late_half]]

    def cur_strip(which, place):
        return line.at[1, place, :, early_half] if which == 0 else line.at[1, :, place, late_half]

    toward = [along_x, along_y]
    place = [row, col]

    def wide_start(which, spots):
        cut = early_half if which == 0 else late_half
        for side_of, device, slot in ((0, before, 2), (1, after, 0)):
            remote(line.at[(1,) + spots + (cut,)], line.at[(slot,) + spots + (cut,)],
                   wide_send.at[side_of], wide_recv.at[side_of], (device, clus)).start()

    for own, send, recv in ((own_cur, cur_send, cur_recv), (own_ray, ray_send, ray_recv)):
        for which in range(2):
            for k in (2, 1, 3):
                remote(own[which], own[which], send.at[0, which], recv.at[which], toward[which](k)).start()
        if own is own_cur:
            wide_start(0, (row, col))
            wide_start(1, (row, col))

    three_ray = [past.at[0, pl.ds(0, side - 1), early_half], past.at[0, pl.ds(0, side - 1), late_half]]
    three_cur = [line.at[1, 0, pl.ds(0, side - 1), early_half], line.at[1, 0, pl.ds(0, side - 1), late_half]]
    strips_ray = [past.at[pl.ds(0, side - 1), :, early_half], past.at[pl.ds(0, side - 1), :, late_half]]
    strips_cur = [line.at[1, pl.ds(0, side - 1), :, early_half], line.at[1, pl.ds(0, side - 1), :, late_half]]

    def waiter(piece, send, recv):
        return remote(piece, piece, send, recv, (slab, clus))

    for which in range(2):
        waiter(three_cur[which], cur_send.at[0, which], cur_recv.at[which]).wait_recv()
        strip = cur_strip(which, place[which])
        for k in (2, 1, 3):
            remote(strip, strip, cur_send.at[1, which], cur_far_recv.at[which, place[which]],
                   toward[1 - which](k)).start()
    for which in range(2):
        waiter(three_ray[which], ray_send.at[0, which], ray_recv.at[which]).wait_recv()
        for k in (2, 1, 3):
            remote(row_ray[which], row_ray[which], ray_send.at[1, which], ray_far_recv.at[which],
                   toward[1 - which](k)).start()
    for which in range(2):
        for k in (1, 3, 2):
            spots = (row, lax.rem(col + k, side)) if which == 0 else (lax.rem(row + k, side), col)
            wide_start(which, spots)

    small[2].wait()
    small[3].wait()
    pltpu.make_async_copy(trans_hbm.at[pl.ds(0, n_slab)], trans, trans_sem).wait()

    def weigh(target, carry):
        wide = trans[target].astype(jnp.float32)
        for q in range(quarters):
            far_weight[pl.ds(target * far_slots, far_slots), q, :] = wide[:, q * LANES:(q + 1) * LANES]
        tags, weights = [], []
        for slot in range(far_slots):
            entry = target * far_slots + slot
            group = far_idx[slot, target * n_clus + clus]
            lag = far_lag[slot, target * n_clus + clus]
            old = lag >= 2
            member = lax.rem(group, n_clus)
            far_at[0, entry] = lax.div(member, side)
            far_at[1, entry] = lax.rem(member, side)
            far_at[2, entry] = jnp.where(old, lags - lag, 0)
            far_mine[entry] = jnp.where(old & (lax.div(group, n_clus) == slab), 1.0, 0.0)
            tag = jnp.where((lag == 1) & (lax.div(group, n_clus) == slab), lax.rem(group, n_clus), -1)
            tags.append(jnp.full((quarters, LANES), tag, jnp.int32))
            weights.append(far_weight[entry])
        for member in range(n_clus):
            total = jnp.zeros((quarters, LANES), jnp.float32)
            for slot in range(far_slots):
                total += jnp.where(tags[slot] == member, weights[slot], 0.0)
            fresh_weight[member, target] = total
        return carry

    lax.fori_loop(0, n_slab, weigh, 0)

    def turn(c, carry):
        for q in range(quarters):
            wide = rays[c, :, pl.ds(q * LANES, LANES)].astype(jnp.float32)
            rays_back[c, pl.ds(q * LANES, LANES), :] = wide.T.astype(jnp.bfloat16)
        return carry

    lax.fori_loop(0, per, turn, 0)

    for n in range(4, 9):
        small[n].wait()

    def locate(c, carry):
        for j in range(slots):
            entry = c * slots + j
            local_idx = jnp.clip(near_idx[c, j] - (slab - 1) * (n_clus * per), 0, 3 * n_clus * per - 1)
            device = lax.div(local_idx, per)
            spot = lax.rem(device, n_clus)
            near_at[0, entry] = lax.div(device, n_clus)
            near_at[1, entry] = lax.div(spot, side)
            near_at[2, entry] = lax.rem(spot, side)
            near_at[3, entry] = lax.rem(local_idx, per)
            near_at[4, entry] = lags - 1 - near_lag[c, j]
            live = j < near_cnt[c]
            near_mix[0, entry] = jnp.where(live, 1.0 - near_frac[c, j], 0.0)
            near_mix[1, entry] = jnp.where(live, near_frac[c, j], 0.0)
        return carry

    lax.fori_loop(0, per, locate, 0)

    def whole_wide(which):
        piece = line.at[0, :, :, pl.ds(0, lags)]
        return waiter(piece, wide_send.at[which], wide_recv.at[which])

    def far_early(step):
        def one(target, carry):
            total = jnp.zeros((quarters, LANES), jnp.float32)
            for slot in range(far_slots):
                entry = target * far_slots + slot
                time = step + far_at[2, entry]
                total += (far_weight[entry] * far_mine[entry]) * past[far_at[0, entry], far_at[1, entry], time]
            early[target] = total
            return carry

        lax.fori_loop(0, n_slab, one, 0)

    def far_send(step):
        totals = [
            jnp.concatenate([early[2 * p], early[2 * p + 1]], axis=0) for p in range(n_slab // 2)
        ]
        for member in range(n_clus):
            one = past[member // side, member % side, lags - 1 + step]
            both = jnp.concatenate([one, one], axis=0)
            for p in range(n_slab // 2):
                totals[p] += jnp.concatenate(
                    [fresh_weight[member, 2 * p], fresh_weight[member, 2 * p + 1]], axis=0) * both
        for p in range(n_slab // 2):
            part_out[step, 2 * p] = totals[p][:quarters]
            part_out[step, 2 * p + 1] = totals[p][quarters:]

        for k in sorted(range(1, n_slab), key=lambda k: -min(k, n_slab - k)):
            target = lax.rem(slab + k, n_slab)
            remote(part_out.at[step, target], part_in.at[step, slab],
                   two_send.at[step], two_recv.at[step], (target, clus)).start()
        part_in[step, slab] = part_out[step, slab]

    for k in (1, 3, 2):
        for which in range(2):
            spot = lax.rem(place[which] + k, side)
            waiter(cur_strip(which, spot), cur_send.at[1, which], cur_far_recv.at[which, spot]).wait_recv()
            wide_start(which, (spot, slice(None)) if which == 0 else (slice(None), spot))
    for which in range(2):
        waiter(strips_ray[which], ray_send.at[1, which], ray_far_recv.at[which]).wait_recv()
    far_early(0)
    far_send(0)

    whole_wide(0).wait_recv()
    whole_wide(1).wait_recv()
    fetch_inverses.wait()
    fetch_near.wait()

    row_id = lax.broadcasted_iota(jnp.int32, (per, 1), 0)

    def whole_one(step):
        return waiter(land.at[step, pl.ds(0, n_clus - 1)], one_send.at[step], one_recv.at[step])

    def whole_spec(step):
        return waiter(land_ray.at[step, pl.ds(0, n_clus - 1)], spec_send.at[step], spec_recv.at[step])

    def whole_fwd(step, which):
        return waiter(land.at[step, pl.ds(0, n_clus)], fwd_send.at[step, which], fwd_recv.at[step, which])

    def whole_two(step):
        return waiter(part_in.at[step, pl.ds(0, n_slab - 1)], two_send.at[step], two_recv.at[step])

    def body(step, carry):
        @pl.when(step > 0)
        def _():
            last = step - 1
            for which, slot in ((0, 2), (1, 0)):
                whole_fwd(last, which).wait_recv()
                for k in range(n_clus):
                    line[slot, k // side, k % side, lags + last] = land[last, slot * n_clus + k]

        def blend_one(c, inner):
            for j in range(slots):
                entry = c * slots + j
                index = (near_at[0, entry], near_at[1, entry], near_at[2, entry])
                sub = near_at[3, entry]
                time = step + near_at[4, entry]
                now, old = near_mix[0, entry], near_mix[1, entry]
                for half in range(2):
                    mixed = (
                        now * line[index + (time + 1, half, pl.ds(sub, 1), slice(None))]
                        + old * line[index + (time, half, pl.ds(sub, 1), slice(None))]
                    )
                    blend[half, pl.ds(entry, 1), :] = mixed.astype(jnp.bfloat16).astype(jnp.float32)
            return inner

        lax.fori_loop(0, per, blend_one, 0)

        def near_one(c, inner):
            for first in range(0, unknowns, CHUNK):
                rows = min(CHUNK, unknowns - first)
                left = jnp.zeros((rows, LANES), jnp.float32)
                right = jnp.zeros((rows, tail), jnp.float32)
                for j in range(slots):
                    entry = c * slots + j
                    left += (near[c, j, pl.ds(first, rows), pl.ds(0, LANES)].astype(jnp.float32)
                             * blend[0, pl.ds(entry, 1), :])
                    right += (near[c, j, pl.ds(first, rows), pl.ds(LANES, tail)].astype(jnp.float32)
                              * blend[1, pl.ds(entry, 1), pl.ds(0, tail)])
                partial[c, pl.ds(first, rows), :] = left + jnp.concatenate(
                    [right, jnp.zeros((rows, LANES - tail), jnp.float32)], axis=1)
            return inner

        lax.fori_loop(0, per, near_one, 0)

        field = jnp.zeros((per, unknowns), jnp.float32)
        for c in range(per):
            pick = jnp.where(row_id == c, 1.0, 0.0) * jnp.ones((per, 2 * LANES), jnp.float32)
            pick = pick.astype(jnp.bfloat16)
            value = partial[c]
            high = value.astype(jnp.bfloat16)
            low = (value - high.astype(jnp.float32)).astype(jnp.bfloat16)
            field += dot(pick, jnp.concatenate([high, low], axis=1), NT)

        whole_two(step).wait_recv()
        incoming[...] = jnp.sum(part_in[step], axis=0)
        spread = jnp.concatenate(
            [shift[:, q * LANES:(q + 1) * LANES] * incoming[pl.ds(q, 1), :] for q in range(quarters)], axis=1)
        for c in range(per):
            field += dot(jnp.where(row_id == c, spread, 0.0).astype(jnp.bfloat16), rays_back[c], NN)
        right_side = (incident[step] - field).astype(jnp.bfloat16).astype(jnp.float32)
        current = jnp.zeros((per, unknowns), jnp.float32)
        for c in range(per):
            current += dot(jnp.where(row_id == c, right_side, 0.0).astype(jnp.bfloat16), inverses[c], NT)
        out[step] = current

        @pl.when(step < steps - 1)
        def _():
            land[step, home, 0] = current[:, :LANES]
            land[step, home, 1] = jnp.concatenate(
                [current[:, LANES:], jnp.zeros((per, LANES - tail), jnp.float32)], axis=1)
            for dy, dx in FAR_FIRST:
                piece = land.at[step, home]
                target = lax.rem(row + dy, side) * side + lax.rem(col + dx, side)
                remote(piece, piece, one_send.at[step], one_recv.at[step], (slab, target)).start()

            rounded = current.astype(jnp.bfloat16).astype(jnp.float32)
            values = jnp.zeros((per, quarters * LANES), jnp.float32)
            for c in range(per):
                values += dot(jnp.where(row_id == c, rounded, 0.0).astype(jnp.bfloat16), rays[c], NN)
            spectrum = jnp.sum(values * shift[...], axis=0, keepdims=True)
            for q in range(quarters):
                land_ray[step, clus, pl.ds(q, 1), :] = spectrum[:, q * LANES:(q + 1) * LANES]

            for dy, dx in FAR_FIRST:
                piece = land_ray.at[step, clus]
                target = lax.rem(row + dy, side) * side + lax.rem(col + dx, side)
                remote(piece, piece, spec_send.at[step], spec_recv.at[step], (slab, target)).start()

            far_early(step + 1)
            whole_one(step).wait_recv()
            piece = land.at[step, pl.ds(n_clus, n_clus)]
            remote(piece, land.at[step, pl.ds(2 * n_clus, n_clus)],
                   fwd_send.at[step, 0], fwd_recv.at[step, 0], (before, clus)).start()
            remote(piece, land.at[step, pl.ds(0, n_clus)],
                   fwd_send.at[step, 1], fwd_recv.at[step, 1], (after, clus)).start()
            whole_spec(step).wait_recv()
            for k in range(n_clus):
                past[k // side, k % side, lags + step] = land_ray[step, k]
            far_send(step + 1)
            for k in range(n_clus):
                line[1, k // side, k % side, lags + step] = land[step, n_clus + k]

        return carry

    lax.fori_loop(0, steps, body, 0)

    for which in range(2):
        waiter(three_ray[which], ray_send.at[0, which], ray_recv.at[which]).wait_send()
        waiter(three_cur[which], cur_send.at[0, which], cur_recv.at[which]).wait_send()
        waiter(strips_ray[which], ray_send.at[1, which], ray_recv.at[which]).wait_send()
        waiter(strips_cur[which], cur_send.at[1, which], cur_recv.at[which]).wait_send()
        whole_wide(which).wait_send()

    def finish(step, carry):
        whole_two(step).wait_send()

        @pl.when(step < steps - 1)
        def _():
            whole_one(step).wait_send()
            whole_spec(step).wait_send()
            whole_fwd(step, 0).wait_send()
            whole_fwd(step, 1).wait_send()

        return carry

    lax.fori_loop(0, steps, finish, 0)


def local(
    incident, history, near_blocks, near_idx, near_cnt, near_lag, near_frac,
    inverses, rays, shift, far_idx, far_lag, trans,
):
    lags, per, unknowns = history.shape
    steps = incident.shape[0]
    slots = near_idx.shape[1]
    far_slots = far_idx.shape[1]
    n_slab = lax.axis_size("slab")
    n_clus = lax.axis_size("clus")
    side = SIDE
    span = lags + steps
    quarters = rays.shape[1] // LANES
    sizes = (steps, lags, n_slab, side, per, slots, unknowns, far_slots)
    vmem = pl.BlockSpec(memory_space=pltpu.VMEM)
    dma = pltpu.SemaphoreType.DMA
    return pl.pallas_call(
        functools.partial(march, sizes),
        out_shape=jax.ShapeDtypeStruct((steps, per, unknowns), jnp.float32),
        in_specs=[pl.BlockSpec(memory_space=pltpu.HBM)] * 13,
        out_specs=vmem,
        scratch_shapes=[
            pltpu.SMEM(near_idx.shape, jnp.int32),
            pltpu.SMEM(near_cnt.shape, jnp.int32),
            pltpu.SMEM(near_lag.shape, jnp.int32),
            pltpu.SMEM(near_frac.shape, jnp.float32),
            pltpu.SMEM((5, per * slots), jnp.int32),
            pltpu.SMEM((2, per * slots), jnp.float32),
            pltpu.SMEM((3, n_slab * far_slots), jnp.int32),
            pltpu.SMEM((n_slab * far_slots,), jnp.float32),
            pltpu.SMEM(far_idx.shape[::-1], jnp.int32),
            pltpu.SMEM(far_lag.shape[::-1], jnp.int32),
            pltpu.VMEM(incident.shape, jnp.float32),
            pltpu.VMEM(history.shape, jnp.float32),
            pltpu.VMEM(shift.shape, jnp.float32),
            pltpu.VMEM(near_blocks.shape, near_blocks.dtype),
            pltpu.VMEM((rays.shape[0],) + rays.shape[:0:-1], rays.dtype),
            pltpu.VMEM(rays.shape, rays.dtype),
            pltpu.VMEM(inverses.shape, inverses.dtype),
            pltpu.VMEM((n_slab,) + trans.shape[1:], trans.dtype),
            pltpu.VMEM((n_slab * far_slots, quarters, LANES), jnp.float32),
            pltpu.VMEM((n_clus, n_slab, quarters, LANES), jnp.float32),
            pltpu.VMEM((3, side, side, span, 2, per, LANES), jnp.float32),
            pltpu.VMEM((side, side, span, quarters, LANES), jnp.float32),
            pltpu.VMEM((steps - 1, 3 * n_clus, 2, per, LANES), jnp.float32),
            pltpu.VMEM((steps - 1, n_clus, quarters, LANES), jnp.float32),
            pltpu.VMEM((steps, n_slab, quarters, LANES), jnp.float32),
            pltpu.VMEM((steps, n_slab, quarters, LANES), jnp.float32),
            pltpu.VMEM((n_slab, quarters, LANES), jnp.float32),
            pltpu.VMEM((2, per * slots, LANES), jnp.float32),
            pltpu.VMEM((per, unknowns, LANES), jnp.float32),
            pltpu.VMEM((quarters, LANES), jnp.float32),
            dma((9,)), dma(()), dma(()), dma(()), dma(()), dma((2, 2)), dma((2,)), dma((2,)), dma((2, 2)), dma((2,)), dma((2, side)), dma((2,)), dma((2,)),
            dma((steps - 1,)), dma((steps - 1,)), dma((steps - 1,)), dma((steps - 1,)), dma((steps - 1, 2)), dma((steps - 1, 2)),
            dma((steps,)), dma((steps,)),
        ],
        compiler_params=pltpu.CompilerParams(
            collective_id=0, has_side_effects=True, vmem_limit_bytes=63 * 1024 * 1024
        ),
    )(
        near_idx, near_cnt, near_lag, near_frac, far_idx.T, far_lag.T,
        incident, history, shift, near_blocks, jnp.swapaxes(rays, 1, 2), inverses, trans,
    )


def solution(mesh):
    split = ("slab", "clus")
    in_specs = (
        P(None, split, None),
        P(None, split, None),
        P(split, None, None, None),
        P(split, None),
        P(split),
        P(split, None),
        P(split, None),
        P(split, None, None),
        P(split, None, None),
        P(split, None),
        P(),
        P(),
        P(),
    )
    return jax.shard_map(local, mesh=mesh, in_specs=in_specs, out_specs=P(None, split, None), check_vma=False)
```
